256 devices in a mesh: section: 16 (over z_hi, y, core), tok: 16 (over z_lo, x).
Axes of the slice: x: 4, y: 4, z: 8 (z_hi: 2, z_lo: 4; z = z_hi * 4 + z_lo), core: 2. Of those that a mesh axis runs over, the one named last changes fastest.
Arguments:
- tokens: bfloat16 [2, 2048, 512], P(None, 'tok'), may hold values from -6 to 6
- offsets: int32 [16], P('section'), may hold values from 1 to 127
- w_qkv: bfloat16 [16, 512, 1536], P('section'), may hold values from -0.25 to 0.25
- w_out: bfloat16 [16, 512, 512], P('section'), may hold values from -0.25 to 0.25
- w_up: bfloat16 [16, 512, 2048], P('section'), may hold values from -0.25 to 0.25
- w_down: bfloat16 [16, 512, 2048], P('section'), may hold values from -0.125 to 0.125
- w_head: bfloat16 [512, 128], replicated, may hold values from -0.25 to 0.25
- era5t: bfloat16 [2, 2048, 128], P(None, 'tok'), may hold values from -6 to 6
- era5: bfloat16 [2, 2048, 128], P(None, 'tok'), may hold values from -6 to 6
- flags: int32 [2, 32], P(None, 'tok'), may hold values 0 or 1
- buckets: int32 [2, 2048], P(None, 'tok'), may hold values from 0 to 7
Outputs:
- grad_qkv: float32 [16, 512, 1536], P('section', 'tok')
- grad_out: float32 [16, 512, 512], P('section', 'tok')
- grad_up: float32 [16, 512, 2048], P('section', 'tok')
- grad_down: float32 [16, 512, 2048], P('section', 'tok')
The draws below stay inside these ranges and needn't reach their ends.
All inputs are finite; a program needn't handle non-finite values. No bound on the sum of `flags` on one device may be relied on, other than what follows from the above.
Results may differ from the reference program's by a relative error of at most 0.029.
Values may be sent and summed in bfloat16 or wider, within the bound.
No kernel may reach another device: no remote copies, remote signals or barrier semaphores. Data moves between devices by JAX's collectives and lax.ppermute only.
A program may use at most 128 MiB of HBM per device.

```python
import math
import jax
import jax.numpy as jnp
from jax import lax

D = 512
FF = 2048
HEAD_DIM = 32
CH = 128
WIN = 128
MICRO = 2
TOK_MB = 128
SLAB = 2048
SAMPLES = 32
N_SECTION = 16
N_TOK = 16


def set_ends(result, own_key, low, top_value):
    longest = result.shape.index(max(result.shape))
    spots = []
    for shift in (0, 1):
        where = [jax.random.randint(jax.random.fold_in(own_key, axis), (), 0, length) for axis, length in enumerate(result.shape)]
        where[longest] = (where[longest] + shift) % result.shape[longest]
        spots.append(tuple(where))
    return result.at[spots[0]].set(low).at[spots[1]].set(top_value)


def block_levels(rng, dims, pieces, low, top_value):
    level, own = 1.0, jax.random.fold_in(rng, 6)
    for position, shards_of in pieces:
        draws = jnp.exp(jax.random.uniform(jax.random.fold_in(own, position), (shards_of,), jnp.float32, low / len(pieces), top_value / len(pieces)))
        level = level * jnp.repeat(draws, dims[position] // shards_of).reshape([-1 if axis == position else 1 for axis in range(len(dims))])
    return level


def bell_draw(rng, dims, scale, limit, split=(), held_as=jnp.bfloat16):
    entries = scale * jax.random.normal(rng, dims, jnp.float32)
    if split:
        entries = entries * block_levels(rng, dims, split, -0.22, 0.18)
    return jnp.clip(entries, -limit, limit).astype(held_as)


def setup_inputs(seed: int = 0) -> dict:
    splits = jax.random.split(jax.random.key(seed), 12)
    return {
        "tokens": bell_draw(splits[0], (MICRO, SLAB, D), 1.0, 6.0, ((1, 16),)),
        "offsets": set_ends(jax.random.randint(splits[1], (N_SECTION,), 1, WIN), jax.random.fold_in(splits[1], 1), 1, WIN - 1).astype(jnp.int32),
        "w_qkv": bell_draw(splits[2], (N_SECTION, D, 3 * D), D ** -0.5, 0.25, ((0, 16),)),
        "w_out": bell_draw(splits[3], (N_SECTION, D, D), D ** -0.5, 0.25, ((0, 16),)),
        "w_up": bell_draw(splits[4], (N_SECTION, D, FF), D ** -0.5, 0.25, ((0, 16),)),
        "w_down": bell_draw(splits[5], (N_SECTION, D, FF), FF ** -0.5, 0.125, ((0, 16),)),
        "w_head": bell_draw(splits[6], (D, CH), D ** -0.5, 0.25),
        "era5t": bell_draw(splits[7], (MICRO, SLAB, CH), 1.0, 6.0, ((1, 16),)),
        "era5": bell_draw(splits[8], (MICRO, SLAB, CH), 1.0, 6.0, ((1, 16),)),
        "flags": set_ends((jax.random.randint(splits[9], (MICRO, SAMPLES), 0, 2) < 1).astype(jnp.int32), jax.random.fold_in(splits[9], 1), 0, 1),
        "buckets": set_ends(jax.random.randint(splits[10], (MICRO, SLAB), 0, 8), jax.random.fold_in(splits[10], 1), 0, 7).astype(jnp.int32),
    }


norm_eps = 1e-05
logit_scale = 10.0
floor_share = 0.75
decay_base = 0.8

def layer_norm(values):
    center = values - lax.optimization_barrier(jnp.mean(values, axis=-1, keepdims=True))
    spread = lax.optimization_barrier(jnp.mean(center * center, axis=-1, keepdims=True))
    return center * lax.rsqrt(spread + norm_eps)

def window_core(packed):
    windows, window_len, triple = packed.shape
    model_width = triple // 3
    head_count = model_width // HEAD_DIM
    queries = packed[:, :, :model_width].reshape(windows, window_len, head_count, HEAD_DIM)
    key_rows = packed[:, :, model_width:2 * model_width].reshape(windows, window_len, head_count, HEAD_DIM)
    values = packed[:, :, 2 * model_width:].reshape(windows, window_len, head_count, HEAD_DIM)
    norm_floor = floor_share * math.sqrt(HEAD_DIM)
    queries = queries / jnp.maximum(jnp.sqrt(lax.optimization_barrier(jnp.sum(queries * queries, axis=-1, keepdims=True))), norm_floor)
    key_rows = key_rows / jnp.maximum(jnp.sqrt(lax.optimization_barrier(jnp.sum(key_rows * key_rows, axis=-1, keepdims=True))), norm_floor)
    scores = logit_scale * jnp.einsum('awhd,avhd->ahwv', queries, key_rows)
    weights = jnp.exp(scores)
    weights = weights / lax.optimization_barrier(jnp.sum(weights, axis=-1, keepdims=True))
    weights = lax.optimization_barrier(weights.astype(jnp.bfloat16)).astype(jnp.float32)
    mixture = jnp.einsum('ahwv,avhd->awhd', weights, values)
    return mixture.reshape(windows, window_len, model_width)

def attend_forward(rows_in, qkv_weight, out_weight):
    row_total, model_width = rows_in.shape
    normed = layer_norm(rows_in.astype(jnp.float32)).astype(jnp.bfloat16)
    packed = jnp.dot(normed, qkv_weight, preferred_element_type=jnp.float32).astype(jnp.bfloat16)
    attended = window_core(packed.astype(jnp.float32).reshape(row_total // WIN, WIN, 3 * model_width))
    attended = attended.reshape(row_total, model_width).astype(jnp.bfloat16)
    mixed_rows = rows_in.astype(jnp.float32) + jnp.dot(attended, out_weight, preferred_element_type=jnp.float32)
    return (normed, packed, attended, mixed_rows)

def attend_backward(normed, packed, grad_rows, qkv_weight, out_weight):
    row_total, model_width = normed.shape
    grad_att = lax.dot_general(grad_rows, out_weight, (((1,), (1,)), ((), ())), preferred_element_type=jnp.float32)
    unused, core_back = jax.vjp(window_core, packed.astype(jnp.float32).reshape(row_total // WIN, WIN, 3 * model_width))
    grad_packed = core_back(grad_att.reshape(row_total // WIN, WIN, model_width))[0]
    grad_packed = grad_packed.reshape(row_total, 3 * model_width).astype(jnp.bfloat16)
    grad_normed = lax.dot_general(grad_packed, qkv_weight, (((1,), (1,)), ((), ())), preferred_element_type=jnp.float32)
    return (grad_normed, grad_packed)

def mlp_pieces(mixed_rows, up_weight):
    normed = layer_norm(mixed_rows).astype(jnp.bfloat16)
    lifted = jnp.dot(normed, up_weight, preferred_element_type=jnp.float32)
    hidden = jax.nn.gelu(lifted).astype(jnp.bfloat16)
    return (normed, lifted, hidden)

def mlp_forward(mixed_rows, up_weight, down_weight):
    normed, lifted, hidden = mlp_pieces(mixed_rows, up_weight)
    product = lax.dot_general(hidden, down_weight, (((1,), (1,)), ((), ())), preferred_element_type=jnp.float32)
    return (mixed_rows + product).astype(jnp.bfloat16)

def mlp_backward(mixed_rows, grad_output, up_weight, down_weight):
    normed, lifted, hidden = mlp_pieces(mixed_rows, up_weight)
    grad_rounded = grad_output.astype(jnp.bfloat16)
    grad_hidden = jnp.dot(grad_rounded, down_weight, preferred_element_type=jnp.float32)
    unused, gelu_back = jax.vjp(jax.nn.gelu, lifted)
    grad_lifted = gelu_back(grad_hidden)[0].astype(jnp.bfloat16)
    grad_normed = lax.dot_general(grad_lifted, up_weight, (((1,), (1,)), ((), ())), preferred_element_type=jnp.float32)
    unused_two, norm_back = jax.vjp(layer_norm, mixed_rows)
    grad_mixed = grad_output + norm_back(grad_normed)[0]
    return (grad_mixed, normed, grad_lifted, hidden, grad_rounded)

def head_gradient(final_rows, head_weight, target, row_decay, loss_scale):
    final_wide = final_rows.astype(jnp.float32)
    normed = layer_norm(final_wide).astype(jnp.bfloat16)
    predicted = jnp.dot(normed, head_weight, preferred_element_type=jnp.float32)
    grad_pred = (row_decay[:, None] * (predicted - target) * loss_scale).astype(jnp.bfloat16)
    grad_normed = lax.dot_general(grad_pred, head_weight, (((1,), (1,)), ((), ())), preferred_element_type=jnp.float32)
    unused, norm_back = jax.vjp(layer_norm, final_wide)
    return norm_back(grad_normed)[0]

def shard_term(left_rows, right_rows):
    left_blocks = left_rows.astype(jnp.float32).reshape(N_TOK, TOK_MB, left_rows.shape[1])
    right_blocks = right_rows.astype(jnp.float32).reshape(N_TOK, TOK_MB, right_rows.shape[1])
    return jnp.einsum('trp,trq->tpq', left_blocks, right_blocks)

def reference(tokens, offsets, w_qkv, w_out, w_up, w_down, w_head, era5t, era5, flags, buckets):
    half_count = N_SECTION // 2
    section_inputs = []
    section_saved = []
    section_outputs = []
    for section_now in range(N_SECTION):
        inputs_now = []
        saved_now = []
        outputs_now = []
        offset_now = offsets[section_now]
        for micro_index in range(MICRO):
            if section_now == 0:
                rows_in = tokens[micro_index]
            elif section_now < half_count:
                rows_in = section_outputs[section_now - 1][micro_index]
            else:
                rows_in = (section_outputs[section_now - 1][micro_index].astype(jnp.float32) + section_outputs[N_SECTION - 1 - section_now][micro_index].astype(jnp.float32)).astype(jnp.bfloat16)
            rolled = jnp.roll(rows_in, -offset_now, axis=0)
            normed, packed, attended, mixed_rolled = attend_forward(rolled, w_qkv[section_now], w_out[section_now])
            mixed_rows = jnp.roll(mixed_rolled, offset_now, axis=0)
            inputs_now.append(rows_in)
            saved_now.append((normed, packed, attended, mixed_rows))
            outputs_now.append(mlp_forward(mixed_rows, w_up[section_now], w_down[section_now]))
        section_inputs.append(inputs_now)
        section_saved.append(saved_now)
        section_outputs.append(outputs_now)
    loss_scale = 1.0 / math.sqrt(MICRO * SLAB)
    grads_next = []
    for micro_index in range(MICRO):
        chosen = jnp.repeat(flags[micro_index], TOK_MB // 2)[:, None] == 1
        target = jnp.where(chosen, era5t[micro_index].astype(jnp.float32), era5[micro_index].astype(jnp.float32))
        row_decay = jnp.power(jnp.float32(decay_base), buckets[micro_index].astype(jnp.float32))
        grads_next.append(head_gradient(section_outputs[N_SECTION - 1][micro_index], w_head, target, row_decay, loss_scale))
    skip_grads = []
    for section_now in range(N_SECTION):
        skip_grads.append([])
    totals = []
    for section_now in range(N_SECTION - 1, -1, -1):
        offset_now = offsets[section_now]
        partial_value = jnp.zeros((N_TOK, D, 4 * D + 2 * FF), jnp.float32)
        following = []
        for micro_index in range(MICRO):
            grad_output = grads_next[micro_index]
            if section_now < half_count:
                grad_output = grad_output + skip_grads[section_now][micro_index].astype(jnp.float32)
            normed, packed, attended, mixed_rows = section_saved[section_now][micro_index]
            grad_mixed, normed_two, grad_lifted, hidden, grad_rounded = mlp_backward(mixed_rows, grad_output, w_up[section_now], w_down[section_now])
            grad_rolled = jnp.roll(grad_mixed, -offset_now, axis=0).astype(jnp.bfloat16)
            grad_normed, grad_packed = attend_backward(normed, packed, grad_rolled, w_qkv[section_now], w_out[section_now])
            rolled = jnp.roll(section_inputs[section_now][micro_index], -offset_now, axis=0)
            unused, norm_back = jax.vjp(layer_norm, rolled.astype(jnp.float32))
            grad_input = grad_mixed + jnp.roll(norm_back(grad_normed)[0], offset_now, axis=0)
            grad_term = jnp.concatenate([shard_term(normed, grad_packed), shard_term(attended, grad_rolled), shard_term(normed_two, grad_lifted), shard_term(grad_rounded, hidden)], axis=2)
            partial_value = partial_value + grad_term
            sent_back = grad_input.astype(jnp.bfloat16)
            following.append(sent_back.astype(jnp.float32))
            if section_now >= half_count:
                skip_grads[N_SECTION - 1 - section_now].append(sent_back)
        grads_next = following
        totals.append(lax.optimization_barrier(jnp.sum(lax.optimization_barrier(partial_value.astype(jnp.bfloat16)).astype(jnp.float32), axis=0)))
    summed = jnp.stack(totals[::-1])
    grad_qkv = summed[:, :, :3 * D]
    grad_out = summed[:, :, 3 * D:4 * D]
    grad_up = summed[:, :, 4 * D:4 * D + FF]
    grad_down = summed[:, :, 4 * D + FF:]
    return (grad_qkv, grad_out, grad_up, grad_down)
```

```python
import math

import jax
import jax.numpy as jnp
from jax import lax
from jax.experimental import pallas as pl
from jax.experimental.pallas import tpu as pltpu
from jax.sharding import PartitionSpec as P

HEAD_DIM = 32
WIN = 128
LANES = 128
GROUP = LANES // HEAD_DIM

norm_eps = 1e-05
logit_scale = 10.0
floor_share = 0.75
decay_base = 0.8
norm_floor = floor_share * math.sqrt(HEAD_DIM)

F32 = jnp.float32
BF16 = jnp.bfloat16
VMEM_LIMIT = 48 * 1024 * 1024

SLOT = 512
X_AT, QKV_AT, LEFT_AT, RIGHT_AT, Z_AT, GX_AT, LOW_SLOTS = 0, 1, 4, 11, 20, 21, 22
LEFT_SLOTS, RIGHT_SLOTS = 7, 9
Y_AT, U_AT, WIDE_SLOTS = 0, 1, 5
LOW_STORE, WIDE_STORE = 224, 112

NN = (((1,), (0,)), ((), ()))
NT = (((1,), (1,)), ((), ()))
TN = (((0,), (0,)), ((), ()))


def dot(left, right, dims=NN):
    return lax.dot_general(left, right, dims, preferred_element_type=F32)


def norm_parts(values):
    center = values - jnp.mean(values, axis=-1, keepdims=True)
    scale = lax.rsqrt(jnp.mean(center * center, axis=-1, keepdims=True) + norm_eps)
    return center * scale, scale


def norm_back(normed, scale, grad):
    grad_mean = jnp.mean(grad, axis=-1, keepdims=True)
    grad_dot = jnp.mean(grad * normed, axis=-1, keepdims=True)
    return scale * (grad - grad_mean - normed * grad_dot)


def joined(first, second, start):
    both = jnp.concatenate([first.astype(F32), second.astype(F32)], axis=0)
    return pltpu.roll(both, lax.rem(2 * WIN - start, 2 * WIN), 0)[:WIN]


def head_sum(values):
    width = values.shape[1]
    rows = lax.broadcasted_iota(jnp.int32, (LANES, LANES), 0) // HEAD_DIM
    cols = lax.broadcasted_iota(jnp.int32, (LANES, LANES), 1) // HEAD_DIM
    same = (rows == cols).astype(BF16)
    high = values.astype(BF16)
    low = (values - high.astype(F32)).astype(BF16)
    parts = []
    for at in range(0, width, LANES):
        parts.append(dot(high[:, at : at + LANES], same) + dot(low[:, at : at + LANES], same))
    return jnp.concatenate(parts, axis=1)


def spread_heads(rows):
    head = lax.broadcasted_iota(jnp.int32, rows.shape, 1) // HEAD_DIM
    zero = jnp.zeros_like(rows)
    return jnp.concatenate([jnp.where(head == h, rows, zero) for h in range(GROUP)], axis=0)


def gather_heads(stacked):
    head = lax.broadcasted_iota(jnp.int32, (WIN, LANES), 1) // HEAD_DIM
    result = stacked[:WIN]
    for h in range(1, GROUP):
        result = jnp.where(head == h, stacked[h * WIN : (h + 1) * WIN], result)
    return result


def unit_rows(rows):
    length = jnp.sqrt(head_sum(rows * rows))
    inverse = 1.0 / jnp.maximum(length, norm_floor)
    return inverse, length > norm_floor


def gelu_parts(lifted):
    root = math.sqrt(2.0 / math.pi)
    square = lifted * lifted
    bend = jnp.tanh(root * lifted * (1.0 + 0.044715 * square))
    return square, bend, root


def weight_views(refs):
    first, up, down = refs
    split = 3 * first.shape[0]
    views = [first.at[:, pl.ds(0, split)], first.at[:, pl.ds(split, first.shape[1] - split)]]
    return views + [up, down]


def fetch(pairs, own, sems):
    for index, (mine, other, into) in enumerate(pairs):

        @pl.when(own == 1)
        def _():
            pltpu.make_async_copy(mine, into, sems.at[index]).start()

        @pl.when(own == 0)
        def _():
            pltpu.make_async_copy(other, into, sems.at[index]).start()

    def arrived(index):
        pltpu.make_async_copy(pairs[index][0], pairs[index][2], sems.at[index]).wait()

    return arrived


def forward_kernel(mode, section, *refs):
    info_ref = refs[0]

    @pl.when(info_ref[section, 2] == 1)
    def _():
        forward_section(mode, section, *refs)


def forward_section(mode, section, *refs):
    refs = list(refs)
    info_ref, cur_ref, nxt_ref = refs[:3]
    refs = refs[3:]
    skip_ref = refs.pop(0) if mode == "skip" else None
    mine, other = weight_views(refs[:3]), weight_views(refs[3:6])
    low_store, wide_store, z_ref = refs[8:11]
    held = refs[11:15]
    x_ref, qkv_ref, left_ref, y_ref, u_ref, sems, out_sems = refs[15:]
    arrived = fetch(list(zip(mine, other, held)), info_ref[section, 1], sems)
    w_qkv, w_out, w_up, w_down = held
    low_base, wide_base = section % 2 * LOW_SLOTS, section % 2 * WIDE_SLOTS
    out_copies = []

    def keep(room, store, at):
        goal = store.at[pl.ds(at, room.shape[0])]
        copy = pltpu.make_async_copy(room, goal, out_sems.at[len(out_copies)])
        copy.start()
        out_copies.append(copy)

    x = joined(cur_ref[...], nxt_ref[...], info_ref[section, 0])
    if mode == "skip":
        x = (x + skip_ref[...].astype(F32)).astype(BF16).astype(F32)
    if mode == "double":
        x = x + x
    x_ref[0] = x.astype(BF16)
    keep(x_ref, low_store, low_base + X_AT)
    n1 = norm_parts(x)[0].astype(BF16)
    left_ref[0] = n1
    arrived(0)
    q, k, v = [dot(n1, w_qkv[:, at : at + SLOT]).astype(BF16) for at in (0, SLOT, 2 * SLOT)]
    qkv_ref[0] = q
    qkv_ref[1] = k
    qkv_ref[2] = v
    keep(qkv_ref, low_store, low_base + QKV_AT)
    q = q.astype(F32)
    k = k.astype(F32)
    qh = (q * (logit_scale * unit_rows(q)[0])).astype(BF16)
    kh = (k * unit_rows(k)[0]).astype(BF16)
    ones = jnp.ones((WIN, LANES), BF16)
    attended = []
    for at in range(0, SLOT, LANES):
        scores = dot(spread_heads(qh[:, at : at + LANES]), kh[:, at : at + LANES], NT)
        weights = jnp.exp(scores).astype(BF16)
        mixed = dot(weights, jnp.concatenate([v[:, at : at + LANES], ones], axis=1))
        attended.append(gather_heads(mixed[:, :LANES] / mixed[:, LANES:]))
    att = jnp.concatenate(attended, axis=1).astype(BF16)
    left_ref[1] = att
    arrived(1)
    y = x + dot(att, w_out[...])
    y_ref[0] = y
    keep(y_ref, wide_store, wide_base + Y_AT)
    n2 = norm_parts(y)[0].astype(BF16)
    left_ref[2] = n2
    arrived(2)
    for index in range(LEFT_SLOTS - 3):
        u = dot(n2, w_up[:, index * SLOT : (index + 1) * SLOT])
        u_ref[index] = u
        bend = gelu_parts(u)[1]
        left_ref[3 + index] = (0.5 * u * (1.0 + bend)).astype(BF16)
    keep(u_ref, wide_store, wide_base + U_AT)
    keep(left_ref, low_store, low_base + LEFT_AT)
    arrived(3)
    z = y
    for index in range(LEFT_SLOTS - 3):
        z = z + dot(left_ref[3 + index], w_down[:, index * SLOT : (index + 1) * SLOT], NT)
    z_ref[...] = z.astype(BF16)
    posted = pltpu.make_async_copy(z_ref, low_store.at[low_base + Z_AT], out_sems.at[5])
    posted.start()
    for copy in out_copies + [posted]:
        copy.wait()


def backward_kernel(mode, last, section, *refs):
    info_ref = refs[0]

    @pl.when(info_ref[section, 2] == 1)
    def _():
        backward_section(mode, last, section, *refs)


def backward_section(mode, last, section, *refs):
    refs = list(refs)
    info_ref = refs.pop(0)
    if mode == "head":
        z_ref, aim_ref, head_ref = refs[:3]
        refs = refs[3:]
    else:
        cur_ref, prv_ref = refs[:2]
        refs = refs[2:]
    skip_ref = refs.pop(0) if mode == "skip" else None
    mine, other = weight_views(refs[:3]), weight_views(refs[3:6])
    low_store, wide_store, gx_ref = refs[8:11]
    held = refs[11:15]
    x_ref, qkv_ref, right_ref, y_ref, u_ref, sems, in_sems, out_sem = refs[15:]
    low_base, wide_base = section % 2 * LOW_SLOTS, section % 2 * WIDE_SLOTS
    in_copies = [
        pltpu.make_async_copy(store.at[pl.ds(at, room.shape[0])], room, in_sems.at[index])
        for index, (room, store, at) in enumerate(
            [
                (x_ref, low_store, low_base + X_AT),
                (y_ref, wide_store, wide_base + Y_AT),
                (u_ref, wide_store, wide_base + U_AT),
                (qkv_ref, low_store, low_base + QKV_AT),
            ]
        )
    ]
    pairs = list(zip(mine, other, held))
    arrived = fetch(pairs[::-1], info_ref[section, 1], sems)
    for index in (2, 1, 3, 0):
        in_copies[index].start()
    w_qkv, w_out, w_up, w_down = held
    hidden_slots = u_ref.shape[0]

    if mode == "head":
        normed, scale = norm_parts(z_ref[...].astype(F32))
        channels = head_ref.shape[1]
        predicted = dot(normed.astype(BF16), head_ref[...])
        target = aim_ref[:, :channels].astype(F32)
        bucket = aim_ref[:, channels:].astype(F32)
        decay = jnp.exp(bucket * math.log(decay_base))
        loss_scale = 1.0 / math.sqrt(2 * 16 * WIN)
        grad_pred = (decay * (predicted - target) * loss_scale).astype(BF16)
        dz = norm_back(normed, scale, dot(grad_pred, head_ref[...], NT))
    else:
        dz = joined(prv_ref[...], cur_ref[...], WIN - info_ref[section, 3])
        if mode == "skip":
            dz = dz + skip_ref[...].astype(F32)
        if mode == "double":
            dz = dz + dz
    g_m = dz.astype(BF16)
    right_ref[4 + hidden_slots] = g_m
    arrived(0)
    in_copies[2].wait()
    for index in range(hidden_slots):
        dh = dot(g_m, w_down[:, index * SLOT : (index + 1) * SLOT])
        u = u_ref[index]
        square, bend, root = gelu_parts(u)
        slope = 0.5 * (1.0 + bend) + (0.5 * root) * u * (1.0 - bend * bend) * (
            1.0 + 3 * 0.044715 * square
        )
        right_ref[4 + index] = (slope * dh).astype(BF16)
    arrived(1)
    dn2 = dot(right_ref[4], w_up[:, :SLOT], NT)
    for index in range(1, hidden_slots):
        dn2 = dn2 + dot(right_ref[4 + index], w_up[:, index * SLOT : (index + 1) * SLOT], NT)
    in_copies[1].wait()
    normed, scale = norm_parts(y_ref[0])
    dy = dz + norm_back(normed, scale, dn2)
    g_a = dy.astype(BF16)
    right_ref[3] = g_a
    arrived(2)
    da = dot(g_a, w_out[...], NT).astype(BF16)

    in_copies[3].wait()
    q = qkv_ref[0].astype(F32)
    k = qkv_ref[1].astype(F32)
    q_inv, q_free = unit_rows(q)
    k_inv, k_free = unit_rows(k)
    qu = q * q_inv
    ku = k * k_inv
    qh = (logit_scale * qu).astype(BF16)
    kh = ku.astype(BF16)
    ones = jnp.ones((WIN, LANES), BF16)
    dq_parts, dk_parts = [], []
    for at in range(0, SLOT, LANES):
        kg = kh[:, at : at + LANES]
        vg = qkv_ref[2, :, at : at + LANES]
        queries = spread_heads(qh[:, at : at + LANES])
        weights = jnp.exp(dot(queries, kg, NT))
        probs = weights / dot(weights.astype(BF16), ones)
        probs_low = probs.astype(BF16)
        grads = spread_heads(da[:, at : at + LANES])
        dp = dot(grads, vg, NT)
        ds = (probs * (dp - dot((probs * dp).astype(BF16), ones))).astype(BF16)
        right_ref[2, :, at : at + LANES] = dot(probs_low, grads, TN).astype(BF16)
        dq_parts.append(gather_heads(dot(ds, kg)))
        dk_parts.append(dot(ds, queries, TN))
    dqh = logit_scale * jnp.concatenate(dq_parts, axis=1)
    dkh = jnp.concatenate(dk_parts, axis=1)
    dq = q_inv * (dqh - jnp.where(q_free, qu * head_sum(qu * dqh), 0.0))
    dk = k_inv * (dkh - jnp.where(k_free, ku * head_sum(ku * dkh), 0.0))
    right_ref[0] = dq.astype(BF16)
    right_ref[1] = dk.astype(BF16)
    right_goal = low_store.at[pl.ds(low_base + RIGHT_AT, RIGHT_SLOTS)]
    out_copy = pltpu.make_async_copy(right_ref, right_goal, out_sem.at[0])
    out_copy.start()
    arrived(3)
    in_copies[0].wait()
    if last:
        gx_ref[...] = g_a
    else:
        dn1 = dot(right_ref[0], w_qkv[:, :SLOT], NT)
        for index in (1, 2):
            dn1 = dn1 + dot(right_ref[index], w_qkv[:, index * SLOT : (index + 1) * SLOT], NT)
        normed, scale = norm_parts(x_ref[0].astype(F32))
        gx_ref[...] = (dy + norm_back(normed, scale, dn1)).astype(BF16)
    posted = pltpu.make_async_copy(gx_ref, low_store.at[low_base + GX_AT], out_sem.at[1])
    posted.start()
    out_copy.wait()
    posted.wait()


def pick_kernel(ranges, *refs):
    store_ref = refs[1]
    outs, sems = refs[2:-1], refs[-1]
    copies = []
    for index, (at, count) in enumerate(ranges):
        source = store_ref.at[pl.ds(at, count)]
        copies.append(pltpu.make_async_copy(source, outs[index], sems.at[index]))
        copies[-1].start()
    for copy in copies:
        copy.wait()


def weight_kernel(inner, *refs):
    info_ref, store_ref = refs[:2]
    received = refs[2:6]
    near_refs, far_refs = refs[6 : 6 + inner], refs[6 + inner : 6 + 2 * inner]
    left, right, room, sems = refs[6 + 2 * inner :]
    copies = []
    for into, at, count, got in ((left, LEFT_AT, LEFT_SLOTS, 0), (right, RIGHT_AT, RIGHT_SLOTS, 1)):
        for index in range(count):
            columns = pl.ds(index * SLOT, SLOT)
            for part in range(2):
                goal = into.at[pl.ds(part * WIN, WIN), columns]
                sem = sems.at[len(copies)]
                for side in range(2):

                    @pl.when(info_ref[0] == side)
                    def _():
                        if part == 0:
                            source = store_ref.at[side * LOW_SLOTS + at + index]
                        else:
                            source = received[2 * got + side].at[index]
                        pltpu.make_async_copy(source, goal, sem).start()

                copies.append(pltpu.make_async_copy(store_ref.at[at + index], goal, sem))
    for copy in copies:
        copy.wait()
    width, step = room.shape
    hidden = right.shape[1] - 5 * width
    total = 4 * width + 2 * hidden
    outer = near_refs[0].shape[0]
    strip = near_refs[0].shape[1]
    split = near_refs[0].shape[2]
    for at in range(0, total, step):
        if at < 3 * width:
            first, second = left[:, :width], right[:, at : at + step]
        elif at < 4 * width:
            first, second = left[:, width : 2 * width], right[:, at : at + step]
        elif at < 4 * width + hidden:
            first, second = left[:, 2 * width : 3 * width], right[:, at : at + step]
        else:
            start = 3 * width + at - 4 * width - hidden
            first, second = right[:, 4 * width + hidden :], left[:, start : start + step]
        room[...] = dot(first, second, TN).astype(BF16)
        for distance in range(inner):
            if at < split:
                column = lax.rem(info_ref[1] + distance, inner)
            else:
                column = lax.rem(info_ref[2] + distance, outer)
            for line in range(outer):
                if at < split:
                    owner = line * inner + column
                    near_refs[distance][line, :, at : at + step] = room[
                        pl.ds(owner * strip, strip), :
                    ]
                else:
                    owner = column * inner + line
                    far_refs[distance][line, :, at - split : at - split + step] = room[
                        pl.ds(owner * strip, strip), :
                    ]


VMEM = pl.BlockSpec(memory_space=pltpu.VMEM)
SMEM = pl.BlockSpec(memory_space=pltpu.SMEM)
HBM = pl.BlockSpec(memory_space=pltpu.HBM)


def body(tokens, offsets, w_qkv, w_out, w_up, w_down, w_head, era5t, era5, flags, buckets):
    section_count = lax.axis_size("section")
    tok_count = lax.axis_size("tok")
    pair_count = section_count // 2
    half_pairs = pair_count // 2
    section_index = lax.axis_index("section")
    tok_index = lax.axis_index("tok")
    pair_index = section_index // 2
    core_index = section_index % 2
    micro_count, row_count, width = tokens.shape
    hidden = w_up.shape[2]
    mine = (jnp.concatenate([w_qkv[0], w_out[0]], axis=1), w_up[0], w_down[0])

    def place(section, tok):
        return section * tok_count + tok % tok_count

    def moved(block, route):
        return lax.ppermute(block, ("section", "tok"), route)

    def hop(block, low_pair, step, tok_shift):
        route = []
        for pair in range(pair_count - 1):
            if pair % 2 == low_pair % 2:
                for core in range(2):
                    for tok in range(tok_count):
                        low, high = 2 * pair + core, 2 * pair + 2 + core
                        origin, goal = (low, high) if step > 0 else (high, low)
                        route.append((place(origin, tok + tok_shift), place(goal, tok)))
        return moved(block, route)

    def along(block, tok_shift, sections):
        route = []
        for section in sections:
            for tok in range(tok_count):
                route.append((place(section, tok + tok_shift), place(section, tok)))
        return moved(block, route)

    def mirror(block, pairs):
        route = []
        for one in pairs:
            for goal in (pair_count - 1 - one,):
                for core in range(2):
                    for tok in range(tok_count):
                        origin = 2 * (pair_count - 1 - goal) + core
                        route.append((place(origin, tok), place(2 * goal + core, tok)))
        return moved(block, sorted(route))

    outer_pairs = [pair for pair in range(pair_count) if pair not in (half_pairs - 1, half_pairs)]

    def swap(block, origins):
        route = [
            (place(section, tok), place(section ^ 1, tok))
            for section in range(section_count)
            if section % 2 in origins
            for tok in range(tok_count)
        ]
        return moved(block, route)

    everyone = range(section_count)
    last_encoder = section_count // 2 - 1
    encoders = range(last_encoder - 1)
    inner_encoders = range(last_encoder - 1, last_encoder + 1)
    inner_decoders = range(last_encoder + 1, last_encoder + 3)
    decoders = range(last_encoder + 3, section_count)

    def far_along(block, blocks, limit, sign, sections):
        bit = 1
        while bit <= limit:
            shifted = along(block, sign * bit, sections)
            block = jnp.where((blocks // bit) % 2 == 1, shifted, block)
            bit *= 2
        return block

    def together(*arrays):
        return lax.optimization_barrier(arrays)

    table = lax.all_gather(offsets, "section").reshape(section_count)
    order = jnp.arange(section_count)
    before = jnp.where(order == 0, 0, jnp.roll(table, 1))
    shifts = (table - before + WIN) % WIN
    start = jnp.sum(jnp.where(order[:, None] >= order[None, :], shifts[None, :], 0), axis=1)

    other = tuple(swap(weight, (0, 1)) for weight in mine)

    info = jnp.stack(
        [
            shifts,
            (core_index == order % 2).astype(jnp.int32),
            (pair_index == order // 2).astype(jnp.int32),
            jnp.roll(shifts, -1),
        ],
        axis=1,
    ).astype(jnp.int32)

    weight_rooms = [
        pltpu.VMEM(weight.shape[1:], BF16) for weight in (w_qkv, w_out, w_up, w_down)
    ]
    weight_sems = pltpu.SemaphoreType.DMA((4,))
    rows_bf = jax.ShapeDtypeStruct((WIN, width), BF16)
    store_shapes = (
        jax.ShapeDtypeStruct((LOW_STORE, WIN, SLOT), BF16),
        jax.ShapeDtypeStruct((WIDE_STORE, WIN, SLOT), F32),
    )
    channels = era5.shape[2]
    hidden_slots = hidden // SLOT

    def room(count, dtype):
        return pltpu.VMEM((count, WIN, SLOT), dtype)

    params = pltpu.CompilerParams(vmem_limit_bytes=VMEM_LIMIT)

    def section_call(kernel, name, inputs, stores, rooms, sems):
        inputs = [info, *inputs]
        first = len(inputs) + 6
        result = pl.pallas_call(
            kernel,
            out_shape=store_shapes + (rows_bf,),
            in_specs=[SMEM] + [VMEM] * (len(inputs) - 1) + [HBM] * 8,
            out_specs=(HBM, HBM, VMEM),
            input_output_aliases={first: 0, first + 1: 1},
            scratch_shapes=weight_rooms
            + rooms
            + [room(1, F32), room(hidden_slots, F32), weight_sems]
            + [pltpu.SemaphoreType.DMA((count,)) for count in sems],
            compiler_params=params,
            name=name,
        )(*inputs, *mine, *other, *stores)
        return tuple(result[:2]), result[2]

    def forward(section, cur, nxt, skip, stores):
        if section < section_count // 2:
            mode = "plain"
        else:
            mode = "double" if section == section_count // 2 else "skip"
        return section_call(
            lambda *refs: forward_kernel(mode, section, *refs),
            "forward_" + mode,
            [cur, nxt] + ([skip] if mode == "skip" else []),
            stores,
            [room(1, BF16), room(3, BF16), room(LEFT_SLOTS, BF16)],
            (6,),
        )

    def backward(section, sources, skip, stores):
        if section == section_count - 1:
            mode = "head"
        elif section >= section_count // 2:
            mode = "plain"
        else:
            mode = "double" if section == section_count // 2 - 1 else "skip"
        return section_call(
            lambda *refs: backward_kernel(mode, section == 0, section, *refs),
            "backward_" + mode,
            [*sources] + ([skip] if mode == "skip" else []),
            stores,
            [room(1, BF16), room(3, BF16), room(RIGHT_SLOTS, BF16)],
            (4, 2),
        )

    def picked(stores, *ranges):
        result = pl.pallas_call(
            lambda *refs: pick_kernel(ranges, *refs),
            out_shape=(store_shapes[0],)
            + tuple(jax.ShapeDtypeStruct((count, WIN, SLOT), BF16) for _, count in ranges),
            in_specs=[HBM],
            out_specs=(HBM,) + (VMEM,) * len(ranges),
            input_output_aliases={0: 0},
            scratch_shapes=[pltpu.SemaphoreType.DMA((len(ranges),))],
            name="pick",
        )(stores[0])
        return (result[0], stores[1]), result[1:]

    def unwritten():
        return pl.pallas_call(
            lambda *refs: None,
            out_shape=store_shapes,
            out_specs=(HBM,) * 2,
            name="unwritten",
        )()

    cur = lax.dynamic_index_in_dim(tokens, core_index, 0, False)
    nxt = along(cur, 1, everyone)
    stores = unwritten()
    chosen = jnp.repeat(
        lax.dynamic_index_in_dim(flags, core_index, 0, False), row_count // flags.shape[1]
    )
    target = jnp.where(
        (chosen == 1)[:, None],
        lax.dynamic_index_in_dim(era5t, core_index, 0, False),
        lax.dynamic_index_in_dim(era5, core_index, 0, False),
    )
    bucket = lax.dynamic_index_in_dim(buckets, core_index, 0, False).astype(BF16)
    bucket = jnp.broadcast_to(bucket[:, None], target.shape)
    aim_here = jnp.stack([target, bucket])

    low_reach = start[section_count - 1 - 2 * pair_index] - start[2 * pair_index]
    high_reach = start[section_count - 2 - 2 * pair_index] - start[2 * pair_index + 1]
    reaches = [jnp.abs(low_reach), jnp.abs(high_reach)]
    reaches_seen = [
        jnp.where(pair_index < half_pairs, reaches[slot], reaches[1 - slot]) for slot in range(2)
    ]
    target_reach = start[section_count - 1]

    def cut(first, second, at):
        return lax.dynamic_slice_in_dim(jnp.concatenate([first, second], axis=0), at, WIN, 0)

    def long_shift(blocks, counts, limit, sign, sections):
        near = far_along(blocks, counts, limit, sign, sections)
        return near, along(near, sign, sections)

    def short_shift(block, count, limit, sign, sections):
        blocks = [block]
        for _ in range(limit + 1):
            blocks.append(along(blocks[-1], sign, sections))
        near, beside = blocks[0], blocks[1]
        for index in range(1, limit + 1):
            near = jnp.where(count == index, blocks[index], near)
            beside = jnp.where(count == index, blocks[index + 1], beside)
        return near, beside

    skips = {}
    aim = None
    for pair in range(pair_count):
        low, high = 2 * pair, 2 * pair + 1
        stores, z_low = forward(low, cur, nxt, skips.get(low), stores)
        nxt = along(z_low, 1, everyone)
        stores, z_high = forward(high, z_low, nxt, skips.get(high), stores)
        if pair < pair_count - 1:
            nxt = hop(z_high, pair, 1, 1)
            cur = hop(z_high, pair, 1, 0)
        if pair == half_pairs - 1:
            reach = start[low + 3] - start[low]
            near, beside = short_shift(
                mirror(z_low, (pair,)), reach // WIN, 2, 1, inner_decoders
            )
            skips[low + 3] = cut(near, beside, reach % WIN)
            cur, nxt, skips[low + 3] = together(cur, nxt, skips[low + 3])
            stores, posts = picked(stores, (Z_AT, 1), (LOW_SLOTS + Z_AT, 1))
            post = jnp.concatenate([jnp.concatenate(posts, axis=0), aim_here], axis=2)
            cur, nxt, post = together(cur, nxt, post)
            counts = [
                jnp.concatenate(
                    [
                        jnp.full((1, 1, width), each // WIN),
                        jnp.full((1, 1, channels), target_reach // WIN),
                    ],
                    axis=2,
                )
                for each in reaches_seen
            ]
            near, beside = long_shift(
                mirror(post, outer_pairs),
                jnp.concatenate(counts, axis=0),
                tok_count - 1,
                1,
                decoders,
            )
            outer_skip = [
                cut(near[slot, :, :width], beside[slot, :, :width], reaches_seen[slot] % WIN)
                for slot in range(2)
            ]
            aim = jnp.concatenate(
                [
                    cut(near[slot, :, width:], beside[slot, :, width:], target_reach % WIN)
                    for slot in range(2)
                ],
                axis=1,
            )
            for goal in range(half_pairs + 1, pair_count):
                skips[2 * goal + 1], skips[2 * goal] = outer_skip

    skips = {}
    sources = (z_high, aim, w_head)
    for pair in range(pair_count - 1, -1, -1):
        low, high = 2 * pair, 2 * pair + 1
        stores, gx_high = backward(high, sources, skips.get(high), stores)
        sources = (gx_high, along(gx_high, -1, everyone))
        stores, gx_low = backward(low, sources, skips.get(low), stores)
        if pair > 0:
            prv = hop(gx_low, pair - 1, -1, -1)
            cur = hop(gx_low, pair - 1, -1, 0)
            sources = (cur, prv)
        if pair == half_pairs:
            reach = start[high] - start[high - 3]
            near, beside = short_shift(
                mirror(gx_high, (pair,)), reach // WIN, 2, -1, inner_encoders
            )
            skips[high - 3] = cut(beside, near, WIN - reach % WIN)
            cur, prv, skips[high - 3] = together(cur, prv, skips[high - 3])
            stores, posts = picked(stores, (LOW_SLOTS + GX_AT, 1), (GX_AT, 1))
            cur, prv, post = together(cur, prv, jnp.concatenate(posts, axis=0))
            sources = (cur, prv)
            counts = jnp.stack([each // WIN for each in reaches_seen])[:, None, None]
            near, beside = long_shift(
                mirror(post, outer_pairs), counts, tok_count - 2, -1, encoders
            )
            outer_skip = [
                cut(beside[slot], near[slot], WIN - reaches_seen[slot] % WIN) for slot in range(2)
            ]
            for goal in range(half_pairs - 1):
                skips[2 * goal], skips[2 * goal + 1] = outer_skip
        if pair == half_pairs - 1:
            stores, lefts = picked(
                stores, (LEFT_AT, LEFT_SLOTS), (LOW_SLOTS + LEFT_AT, LEFT_SLOTS)
            )
            left_low = swap(lefts[0], (1,))
            left_high = swap(lefts[1], (0,))
            cur, prv, left_low, left_high = together(cur, prv, left_low, left_high)
            sources = (cur, prv)

    stores, rights = picked(
        stores, (RIGHT_AT, RIGHT_SLOTS), (LOW_SLOTS + RIGHT_AT, RIGHT_SLOTS)
    )
    right_high = swap(rights[1], (0,))
    right_low = swap(rights[0], (1,))
    total = 4 * width + 2 * hidden
    inner = 4
    outer = tok_count // inner
    strip = width // tok_count
    split = 4 * width + hidden
    tok_in, tok_out = tok_index % inner, tok_index // inner
    step = width
    parts = pl.pallas_call(
        lambda *refs: weight_kernel(inner, *refs),
        out_shape=[jax.ShapeDtypeStruct((outer, strip, split), BF16)] * inner
        + [jax.ShapeDtypeStruct((inner, strip, total - split), BF16)] * outer,
        in_specs=[SMEM] + [HBM] * 5,
        out_specs=[VMEM] * (inner + outer),
        scratch_shapes=[
            pltpu.VMEM((2 * WIN, LEFT_SLOTS * SLOT), BF16),
            pltpu.VMEM((2 * WIN, RIGHT_SLOTS * SLOT), BF16),
            pltpu.VMEM((width, step), BF16),
            pltpu.SemaphoreType.DMA((2 * (LEFT_SLOTS + RIGHT_SLOTS),)),
        ],
        compiler_params=params,
        name="weight_grads",
    )(
        jnp.stack([core_index, tok_in, tok_out]).astype(jnp.int32),
        stores[0],
        left_low,
        left_high,
        right_low,
        right_high,
    )
    near_parts, far_parts = parts[:inner], parts[inner:]

    def ring(block, distance, inside):
        route = []
        for tok in range(tok_count):
            far, near = tok // inner, tok % inner
            if inside:
                goal = far * inner + (near + distance) % inner
            else:
                goal = (far + distance) % outer * inner + near
            route.append((tok, goal))
        return lax.ppermute(block, "tok", route)

    def piece(array, index):
        return lax.dynamic_index_in_dim(array, index, 0, False)

    def first_stage(pieces, inside):
        summed = pieces[0].astype(F32)
        for distance in range(1, len(pieces)):
            summed = summed + ring(pieces[distance], distance, inside).astype(F32)
        return summed.astype(BF16)

    def second_stage(summed, position, size, inside):
        result = piece(summed, position).astype(F32)
        for distance in range(1, size):
            sent = piece(summed, (position + distance) % size)
            result = result + ring(sent, distance, inside).astype(F32)
        return result

    near_sums = first_stage(near_parts, True)
    far_sums = first_stage(far_parts, False)
    near_sums, far_sums = together(near_sums, far_sums)
    near_result = second_stage(near_sums, tok_out, outer, False)
    far_result = second_stage(far_sums, tok_in, inner, True)
    grad_qkv = near_result[:, : 3 * width][None]
    grad_out = near_result[:, 3 * width : 4 * width][None]
    grad_up = near_result[:, 4 * width :][None]
    grad_down = far_result[None]
    return (grad_qkv, grad_out, grad_up, grad_down)


def solution(mesh):
    placed = (
        P(None, "tok", None),
        P("section"),
        P("section", None, None),
        P("section", None, None),
        P("section", None, None),
        P("section", None, None),
        P(),
        P(None, "tok", None),
        P(None, "tok", None),
        P(None, "tok"),
        P(None, "tok"),
    )
    return jax.shard_map(
        body,
        mesh=mesh,
        in_specs=placed,
        out_specs=(
            P("section", "tok", None),
            P("section", "tok", None),
            P("section", "tok", None),
            P("section", "tok", None),
        ),
        check_vma=False,
    )
```

```python
import math

import jax
import jax.numpy as jnp
from jax import lax
from jax.experimental import pallas as pl
from jax.experimental.pallas import tpu as pltpu
from jax.sharding import PartitionSpec as P

HEAD_DIM = 32
WIN = 128
LANES = 128
GROUP = LANES // HEAD_DIM

norm_eps = 1e-05
logit_scale = 10.0
floor_share = 0.75
decay_base = 0.8
norm_floor = floor_share * math.sqrt(HEAD_DIM)

F32 = jnp.float32
BF16 = jnp.bfloat16
VMEM_LIMIT = 48 * 1024 * 1024

SLOT = 512
X_AT, QKV_AT, LEFT_AT, RIGHT_AT, Z_AT, GX_AT, LOW_SLOTS = 0, 1, 4, 11, 20, 21, 22
LEFT_SLOTS, RIGHT_SLOTS = 7, 9
Y_AT, U_AT, WIDE_SLOTS = 0, 1, 5
LOW_STORE, WIDE_STORE = 224, 112

NN = (((1,), (0,)), ((), ()))
NT = (((1,), (1,)), ((), ()))
TN = (((0,), (0,)), ((), ()))


def dot(left, right, dims=NN):
    return lax.dot_general(left, right, dims, preferred_element_type=F32)


def norm_parts(values):
    center = values - jnp.mean(values, axis=-1, keepdims=True)
    scale = lax.rsqrt(jnp.mean(center * center, axis=-1, keepdims=True) + norm_eps)
    return center * scale, scale


def norm_back(normed, scale, grad):
    grad_mean = jnp.mean(grad, axis=-1, keepdims=True)
    grad_dot = jnp.mean(grad * normed, axis=-1, keepdims=True)
    return scale * (grad - grad_mean - normed * grad_dot)


def joined(first, second, start):
    both = jnp.concatenate([first.astype(F32), second.astype(F32)], axis=0)
    return pltpu.roll(both, lax.rem(2 * WIN - start, 2 * WIN), 0)[:WIN]


def head_sum(values):
    width = values.shape[1]
    rows = lax.broadcasted_iota(jnp.int32, (LANES, LANES), 0) // HEAD_DIM
    cols = lax.broadcasted_iota(jnp.int32, (LANES, LANES), 1) // HEAD_DIM
    same = (rows == cols).astype(BF16)
    high = values.astype(BF16)
    low = (values - high.astype(F32)).astype(BF16)
    parts = []
    for at in range(0, width, LANES):
        parts.append(dot(high[:, at : at + LANES], same) + dot(low[:, at : at + LANES], same))
    return jnp.concatenate(parts, axis=1)


def spread_heads(rows):
    head = lax.broadcasted_iota(jnp.int32, rows.shape, 1) // HEAD_DIM
    zero = jnp.zeros_like(rows)
    return jnp.concatenate([jnp.where(head == h, rows, zero) for h in range(GROUP)], axis=0)


def gather_heads(stacked):
    head = lax.broadcasted_iota(jnp.int32, (WIN, LANES), 1) // HEAD_DIM
    result = stacked[:WIN]
    for h in range(1, GROUP):
        result = jnp.where(head == h, stacked[h * WIN : (h + 1) * WIN], result)
    return result


def unit_rows(rows):
    length = jnp.sqrt(head_sum(rows * rows))
    inverse = 1.0 / jnp.maximum(length, norm_floor)
    return inverse, length > norm_floor


def gelu_parts(lifted):
    root = math.sqrt(2.0 / math.pi)
    square = lifted * lifted
    bend = jnp.tanh(root * lifted * (1.0 + 0.044715 * square))
    return square, bend, root


def weight_views(refs):
    first, up, down = refs
    split = 3 * first.shape[0]
    views = [first.at[:, pl.ds(0, split)], first.at[:, pl.ds(split, first.shape[1] - split)]]
    return views + [up, down]


def fetch(pairs, own, sems):
    for index, (mine, other, into) in enumerate(pairs):

        @pl.when(own == 1)
        def _():
            pltpu.make_async_copy(mine, into, sems.at[index]).start()

        @pl.when(own == 0)
        def _():
            pltpu.make_async_copy(other, into, sems.at[index]).start()

    def arrived(index):
        pltpu.make_async_copy(pairs[index][0], pairs[index][2], sems.at[index]).wait()

    return arrived


def forward_kernel(mode, section, *refs):
    info_ref = refs[0]

    @pl.when(info_ref[section, 2] == 1)
    def _():
        forward_section(mode, section, *refs)


def forward_section(mode, section, *refs):
    refs = list(refs)
    info_ref, first_ref, second_ref = refs[:3]
    refs = refs[3:]
    skip_ref = refs.pop(0) if mode == "skip" else None
    mine, other = weight_views(refs[:3]), weight_views(refs[3:6])
    low_store, wide_store, z_ref = refs[8:11]
    held = refs[11:15]
    x_ref, qkv_ref, left_ref, y_ref, u_ref, sems, out_sems = refs[15:]
    arrived = fetch(list(zip(mine, other, held)), info_ref[section, 1], sems)
    w_qkv, w_out, w_up, w_down = held
    low_base, wide_base = section % 2 * LOW_SLOTS, section % 2 * WIDE_SLOTS
    out_copies = []

    def keep(room, store, at):
        goal = store.at[pl.ds(at, room.shape[0])]
        copy = pltpu.make_async_copy(room, goal, out_sems.at[len(out_copies)])
        copy.start()
        out_copies.append(copy)

    x = joined(first_ref[...], second_ref[...], info_ref[section, 0])
    if mode == "skip":
        x = (x + skip_ref[...].astype(F32)).astype(BF16).astype(F32)
    if mode == "double":
        x = x + x
    x_ref[0] = x.astype(BF16)
    keep(x_ref, low_store, low_base + X_AT)
    n1 = norm_parts(x)[0].astype(BF16)
    left_ref[0] = n1
    arrived(0)
    q, k, v = [dot(n1, w_qkv[:, at : at + SLOT]).astype(BF16) for at in (0, SLOT, 2 * SLOT)]
    qkv_ref[0] = q
    qkv_ref[1] = k
    qkv_ref[2] = v
    keep(qkv_ref, low_store, low_base + QKV_AT)
    q = q.astype(F32)
    k = k.astype(F32)
    qh = (q * (logit_scale * unit_rows(q)[0])).astype(BF16)
    kh = (k * unit_rows(k)[0]).astype(BF16)
    ones = jnp.ones((WIN, LANES), BF16)
    attended = []
    for at in range(0, SLOT, LANES):
        scores = dot(spread_heads(qh[:, at : at + LANES]), kh[:, at : at + LANES], NT)
        weights = jnp.exp(scores).astype(BF16)
        mixed = dot(weights, jnp.concatenate([v[:, at : at + LANES], ones], axis=1))
        attended.append(gather_heads(mixed[:, :LANES] / mixed[:, LANES:]))
    att = jnp.concatenate(attended, axis=1).astype(BF16)
    left_ref[1] = att
    arrived(1)
    y = x + dot(att, w_out[...])
    y_ref[0] = y
    keep(y_ref, wide_store, wide_base + Y_AT)
    n2 = norm_parts(y)[0].astype(BF16)
    left_ref[2] = n2
    arrived(2)
    for index in range(LEFT_SLOTS - 3):
        u = dot(n2, w_up[:, index * SLOT : (index + 1) * SLOT])
        u_ref[index] = u
        bend = gelu_parts(u)[1]
        left_ref[3 + index] = (0.5 * u * (1.0 + bend)).astype(BF16)
    keep(u_ref, wide_store, wide_base + U_AT)
    keep(left_ref, low_store, low_base + LEFT_AT)
    arrived(3)
    z = y
    for index in range(LEFT_SLOTS - 3):
        z = z + dot(left_ref[3 + index], w_down[:, index * SLOT : (index + 1) * SLOT], NT)
    z_ref[...] = z.astype(BF16)
    posted = pltpu.make_async_copy(z_ref, low_store.at[low_base + Z_AT], out_sems.at[5])
    posted.start()
    for copy in out_copies + [posted]:
        copy.wait()


def backward_kernel(mode, last, section, *refs):
    info_ref = refs[0]

    @pl.when(info_ref[section, 2] == 1)
    def _():
        backward_section(mode, last, section, *refs)


def backward_section(mode, last, section, *refs):
    refs = list(refs)
    info_ref = refs.pop(0)
    if mode == "head":
        z_ref, aim_ref, head_ref = refs[:3]
        refs = refs[3:]
    else:
        first_ref, second_ref = refs[:2]
        refs = refs[2:]
    skip_ref = refs.pop(0) if mode == "skip" else None
    mine, other = weight_views(refs[:3]), weight_views(refs[3:6])
    low_store, wide_store, gx_ref = refs[8:11]
    held = refs[11:15]
    x_ref, qkv_ref, right_ref, y_ref, u_ref, sems, in_sems, out_sem = refs[15:]
    low_base, wide_base = section % 2 * LOW_SLOTS, section % 2 * WIDE_SLOTS
    in_copies = [
        pltpu.make_async_copy(store.at[pl.ds(at, room.shape[0])], room, in_sems.at[index])
        for index, (room, store, at) in enumerate(
            [
                (x_ref, low_store, low_base + X_AT),
                (y_ref, wide_store, wide_base + Y_AT),
                (u_ref, wide_store, wide_base + U_AT),
                (qkv_ref, low_store, low_base + QKV_AT),
            ]
        )
    ]
    pairs = list(zip(mine, other, held))
    arrived = fetch(pairs[::-1], info_ref[section, 1], sems)
    for index in (2, 1, 3, 0):
        in_copies[index].start()
    w_qkv, w_out, w_up, w_down = held
    hidden_slots = u_ref.shape[0]

    if mode == "head":
        normed, scale = norm_parts(z_ref[...].astype(F32))
        channels = head_ref.shape[1]
        predicted = dot(normed.astype(BF16), head_ref[...])
        target = aim_ref[:, :channels].astype(F32)
        bucket = aim_ref[:, channels:].astype(F32)
        decay = jnp.exp(bucket * math.log(decay_base))
        loss_scale = 1.0 / math.sqrt(2 * 16 * WIN)
        grad_pred = (decay * (predicted - target) * loss_scale).astype(BF16)
        dz = norm_back(normed, scale, dot(grad_pred, head_ref[...], NT))
    else:
        dz = joined(first_ref[...], second_ref[...], info_ref[section, 3])
        if mode == "skip":
            dz = dz + skip_ref[...].astype(F32)
        if mode == "double":
            dz = dz + dz
    g_m = dz.astype(BF16)
    right_ref[4 + hidden_slots] = g_m
    arrived(0)
    in_copies[2].wait()
    for index in range(hidden_slots):
        dh = dot(g_m, w_down[:, index * SLOT : (index + 1) * SLOT])
        u = u_ref[index]
        square, bend, root = gelu_parts(u)
        slope = 0.5 * (1.0 + bend) + (0.5 * root) * u * (1.0 - bend * bend) * (
            1.0 + 3 * 0.044715 * square
        )
        right_ref[4 + index] = (slope * dh).astype(BF16)
    arrived(1)
    dn2 = dot(right_ref[4], w_up[:, :SLOT], NT)
    for index in range(1, hidden_slots):
        dn2 = dn2 + dot(right_ref[4 + index], w_up[:, index * SLOT : (index + 1) * SLOT], NT)
    in_copies[1].wait()
    normed, scale = norm_parts(y_ref[0])
    dy = dz + norm_back(normed, scale, dn2)
    g_a = dy.astype(BF16)
    right_ref[3] = g_a
    arrived(2)
    da = dot(g_a, w_out[...], NT).astype(BF16)

    in_copies[3].wait()
    q = qkv_ref[0].astype(F32)
    k = qkv_ref[1].astype(F32)
    q_inv, q_free = unit_rows(q)
    k_inv, k_free = unit_rows(k)
    qu = q * q_inv
    ku = k * k_inv
    qh = (logit_scale * qu).astype(BF16)
    kh = ku.astype(BF16)
    ones = jnp.ones((WIN, LANES), BF16)
    dq_parts, dk_parts = [], []
    for at in range(0, SLOT, LANES):
        kg = kh[:, at : at + LANES]
        vg = qkv_ref[2, :, at : at + LANES]
        queries = spread_heads(qh[:, at : at + LANES])
        weights = jnp.exp(dot(queries, kg, NT))
        probs = weights / dot(weights.astype(BF16), ones)
        probs_low = probs.astype(BF16)
        grads = spread_heads(da[:, at : at + LANES])
        dp = dot(grads, vg, NT)
        ds = (probs * (dp - dot((probs * dp).astype(BF16), ones))).astype(BF16)
        right_ref[2, :, at : at + LANES] = dot(probs_low, grads, TN).astype(BF16)
        dq_parts.append(gather_heads(dot(ds, kg)))
        dk_parts.append(dot(ds, queries, TN))
    dqh = logit_scale * jnp.concatenate(dq_parts, axis=1)
    dkh = jnp.concatenate(dk_parts, axis=1)
    dq = q_inv * (dqh - jnp.where(q_free, qu * head_sum(qu * dqh), 0.0))
    dk = k_inv * (dkh - jnp.where(k_free, ku * head_sum(ku * dkh), 0.0))
    right_ref[0] = dq.astype(BF16)
    right_ref[1] = dk.astype(BF16)
    right_goal = low_store.at[pl.ds(low_base + RIGHT_AT, RIGHT_SLOTS)]
    out_copy = pltpu.make_async_copy(right_ref, right_goal, out_sem.at[0])
    out_copy.start()
    arrived(3)
    in_copies[0].wait()
    if last:
        gx_ref[...] = g_a
    else:
        dn1 = dot(right_ref[0], w_qkv[:, :SLOT], NT)
        for index in (1, 2):
            dn1 = dn1 + dot(right_ref[index], w_qkv[:, index * SLOT : (index + 1) * SLOT], NT)
        normed, scale = norm_parts(x_ref[0].astype(F32))
        gx_ref[...] = (dy + norm_back(normed, scale, dn1)).astype(BF16)
    posted = pltpu.make_async_copy(gx_ref, low_store.at[low_base + GX_AT], out_sem.at[1])
    posted.start()
    out_copy.wait()
    posted.wait()


def pick_kernel(ranges, *refs):
    core_ref, store_ref = refs[:2]
    outs, sems = refs[3:-1], refs[-1]
    copies = []
    for index, (at, count, given) in enumerate(ranges):
        base = at + (1 - core_ref[0]) * LOW_SLOTS if given else at
        source = store_ref.at[pl.ds(base, count)]
        copies.append(pltpu.make_async_copy(source, outs[index], sems.at[index]))
        copies[-1].start()
    for copy in copies:
        copy.wait()


def weight_kernel(inner, *refs):
    info_ref, store_ref = refs[:2]
    received = refs[2:4]
    groups = [refs[4 + group * inner : 4 + (group + 1) * inner] for group in range(3)]
    left, right, room, sems = refs[4 + 3 * inner :]
    copies = []
    for into, at, count, got in ((left, LEFT_AT, LEFT_SLOTS, 0), (right, RIGHT_AT, RIGHT_SLOTS, 1)):
        for index in range(count):
            columns = pl.ds(index * SLOT, SLOT)
            for part in range(2):
                goal = into.at[pl.ds(part * WIN, WIN), columns]
                sem = sems.at[len(copies)]
                if part == 0:
                    source = store_ref.at[info_ref[0] * LOW_SLOTS + at + index]
                else:
                    source = received[got].at[index]
                copies.append(pltpu.make_async_copy(source, goal, sem))
                copies[-1].start()
    for copy in copies:
        copy.wait()
    width, step = room.shape
    hidden = right.shape[1] - 5 * width
    total = 4 * width + 2 * hidden
    outer, strip, group_width = groups[0][0].shape
    for at in range(0, total, step):
        if at < 3 * width:
            first, second = left[:, :width], right[:, at : at + step]
        elif at < 4 * width:
            first, second = left[:, width : 2 * width], right[:, at : at + step]
        elif at < 4 * width + hidden:
            first, second = left[:, 2 * width : 3 * width], right[:, at : at + step]
        else:
            start = 3 * width + at - 4 * width - hidden
            first, second = right[:, 4 * width + hidden :], left[:, start : start + step]
        room[...] = dot(first, second, TN).astype(BF16)
        group = at // group_width
        columns = slice(at % group_width, at % group_width + step)
        for distance in range(inner):
            place = lax.rem(info_ref[1 if group < 2 else 2] + distance, inner)
            for line in range(outer):
                owner = line * inner + place if group < 2 else place * inner + line
                groups[group][distance][line, :, columns] = room[pl.ds(owner * strip, strip), :]


VMEM = pl.BlockSpec(memory_space=pltpu.VMEM)
SMEM = pl.BlockSpec(memory_space=pltpu.SMEM)
HBM = pl.BlockSpec(memory_space=pltpu.HBM)


def body(tokens, offsets, w_qkv, w_out, w_up, w_down, w_head, era5t, era5, flags, buckets):
    section_count = lax.axis_size("section")
    tok_count = lax.axis_size("tok")
    pair_count = section_count // 2
    half_pairs = pair_count // 2
    section_index = lax.axis_index("section")
    tok_index = lax.axis_index("tok")
    pair_index = section_index // 2
    core_index = section_index % 2
    micro_count, row_count, width = tokens.shape
    hidden = w_up.shape[2]
    mine = (jnp.concatenate([w_qkv[0], w_out[0]], axis=1), w_up[0], w_down[0])

    def place(section, tok):
        return section * tok_count + tok % tok_count

    def moved(block, route):
        return lax.ppermute(block, ("section", "tok"), route)

    def hop(block, low_pair, step, tok_shift):
        middle = half_pairs - 1
        route = []
        for pair in range(pair_count - 1):
            if (pair > middle) - (pair < middle) == (low_pair > middle) - (low_pair < middle):
                for core in range(2):
                    for tok in range(tok_count):
                        low, high = 2 * pair + core, 2 * pair + 2 + core
                        origin, goal = (low, high) if step > 0 else (high, low)
                        route.append((place(origin, tok + tok_shift), place(goal, tok)))
        return moved(block, sorted(route))

    def along(block, tok_shift, sections):
        route = []
        for section in sections:
            for tok in range(tok_count):
                route.append((place(section, tok + tok_shift), place(section, tok)))
        return moved(block, route)

    def swap(block):
        route = [
            (place(section, tok), place(section ^ 1, tok))
            for section in range(section_count)
            for tok in range(tok_count)
        ]
        return moved(block, route)

    def across(block, pairs, offsets, sign):
        blocks = []
        for offset in offsets:
            route = []
            for pair in pairs:
                shift = offset * sign if pair < half_pairs else -offset * sign
                for core in range(2):
                    for tok in range(tok_count):
                        goal = place(2 * (pair_count - 1 - pair) + core, tok)
                        route.append((place(2 * pair + core, tok + shift), goal))
            blocks.append(moved(block, sorted(route)))
        return blocks

    everyone = range(section_count)
    def far_along(blocks, counts):
        bit = 1
        while bit < tok_count:
            shifted = along(blocks, bit, everyone)
            blocks = jnp.where((counts % tok_count // bit) % 2 == 1, shifted, blocks)
            bit *= 2
        return blocks

    def together(*arrays):
        return lax.optimization_barrier(arrays)

    table = lax.all_gather(offsets, "section").reshape(section_count)
    order = jnp.arange(section_count)
    before = jnp.where(order == 0, 0, jnp.roll(table, 1))
    turn = section_count // 2
    moves = jnp.where(
        order <= turn, (table - before + WIN) % WIN, -((before - table + WIN) % WIN)
    )
    start = jnp.sum(jnp.where(order[:, None] >= order[None, :], moves[None, :], 0), axis=1)

    other = [swap(weight) for weight in mine]

    info = jnp.stack(
        [
            jnp.where(order <= turn, moves, WIN + moves),
            (core_index == order % 2).astype(jnp.int32),
            (pair_index == order // 2).astype(jnp.int32),
            jnp.roll(jnp.where(order <= turn, WIN - moves, -moves), -1),
        ],
        axis=1,
    ).astype(jnp.int32)

    weight_rooms = [
        pltpu.VMEM(weight.shape[1:], BF16) for weight in (w_qkv, w_out, w_up, w_down)
    ]
    weight_sems = pltpu.SemaphoreType.DMA((4,))
    rows_bf = jax.ShapeDtypeStruct((WIN, width), BF16)
    store_shapes = (
        jax.ShapeDtypeStruct((LOW_STORE, WIN, SLOT), BF16),
        jax.ShapeDtypeStruct((WIDE_STORE, WIN, SLOT), F32),
    )
    channels = era5.shape[2]
    hidden_slots = hidden // SLOT

    def room(count, dtype):
        return pltpu.VMEM((count, WIN, SLOT), dtype)

    params = pltpu.CompilerParams(vmem_limit_bytes=VMEM_LIMIT)

    def section_call(kernel, name, inputs, stores, rooms, sems):
        inputs = [info, *inputs]
        first = len(inputs) + 6
        result = pl.pallas_call(
            kernel,
            out_shape=store_shapes + (rows_bf,),
            in_specs=[SMEM] + [VMEM] * (len(inputs) - 1) + [HBM] * 8,
            out_specs=(HBM, HBM, VMEM),
            input_output_aliases={first: 0, first + 1: 1},
            scratch_shapes=weight_rooms
            + rooms
            + [room(1, F32), room(hidden_slots, F32), weight_sems]
            + [pltpu.SemaphoreType.DMA((count,)) for count in sems],
            compiler_params=params,
            name=name,
        )(*inputs, *mine, *other, *stores)
        return tuple(result[:2]), result[2]

    def forward(section, sources, skip, stores):
        if section < section_count // 2:
            mode = "plain"
        else:
            mode = "double" if section == section_count // 2 else "skip"
        return section_call(
            lambda *refs: forward_kernel(mode, section, *refs),
            "forward_" + mode,
            [*sources] + ([skip] if mode == "skip" else []),
            stores,
            [room(1, BF16), room(3, BF16), room(LEFT_SLOTS, BF16)],
            (6,),
        )

    def backward(section, sources, skip, stores):
        if section == section_count - 1:
            mode = "head"
        elif section >= section_count // 2:
            mode = "plain"
        else:
            mode = "double" if section == section_count // 2 - 1 else "skip"
        return section_call(
            lambda *refs: backward_kernel(mode, section == 0, section, *refs),
            "backward_" + mode,
            [*sources] + ([skip] if mode == "skip" else []),
            stores,
            [room(1, BF16), room(3, BF16), room(RIGHT_SLOTS, BF16)],
            (4, 2),
        )

    core_scalar = core_index[None].astype(jnp.int32)

    def picked(stores, *ranges):
        result = pl.pallas_call(
            lambda *refs: pick_kernel(ranges, *refs),
            out_shape=(store_shapes[0],)
            + tuple(jax.ShapeDtypeStruct((count, WIN, SLOT), BF16) for _, count, _ in ranges),
            in_specs=[SMEM, HBM],
            out_specs=(HBM,) + (VMEM,) * len(ranges),
            input_output_aliases={1: 0},
            scratch_shapes=[pltpu.SemaphoreType.DMA((len(ranges),))],
            name="pick",
        )(core_scalar, stores[0])
        return (result[0], stores[1]), result[1:]

    def unwritten():
        return pl.pallas_call(
            lambda *refs: None,
            out_shape=store_shapes,
            out_specs=(HBM,) * 2,
            name="unwritten",
        )()

    cur = lax.dynamic_index_in_dim(tokens, core_index, 0, False)
    sources = (cur, along(cur, 1, everyone))
    stores = unwritten()
    chosen = jnp.repeat(
        lax.dynamic_index_in_dim(flags, core_index, 0, False), row_count // flags.shape[1]
    )
    target = jnp.where(
        (chosen == 1)[:, None],
        lax.dynamic_index_in_dim(era5t, core_index, 0, False),
        lax.dynamic_index_in_dim(era5, core_index, 0, False),
    )
    bucket = lax.dynamic_index_in_dim(buckets, core_index, 0, False).astype(BF16)
    bucket = jnp.broadcast_to(bucket[:, None], target.shape)
    aims = lax.all_gather(jnp.concatenate([target, bucket], axis=1), "tok", axis=0, tiled=True)
    slab = tok_count * row_count
    aims = jnp.concatenate([aims, aims[:WIN]], axis=0)
    first_row = (tok_index * row_count + start[section_count - 1] + 2 * slab) % slab
    aim = lax.dynamic_slice_in_dim(aims, first_row, WIN, 0)

    outer = jnp.arange(2 * (half_pairs - 1))
    reaches = start[section_count - 1 - outer] - start[outer]
    nearer = jnp.minimum(pair_index, pair_count - 1 - pair_index)
    own = [
        start[section_count - 1 - 2 * nearer - slot] - start[2 * nearer + slot] for slot in range(2)
    ]
    outer_encoders = range(half_pairs - 1)
    outer_pairs = [*outer_encoders, *range(half_pairs + 1, pair_count)]
    lowest, beyond = -2, 3

    def between(blocks, lowest, reach):
        count = jnp.floor_divide(reach, WIN)
        near, beside = blocks[0], blocks[1]
        for index in range(1, len(blocks) - 1):
            near = jnp.where(count == lowest + index, blocks[index], near)
            beside = jnp.where(count == lowest + index, blocks[index + 1], beside)
        both = jnp.concatenate([near, beside], axis=0)
        return lax.dynamic_slice_in_dim(both, reach % WIN, WIN, 0)

    def outer_skips(stores, places, sign):
        stores, posts = picked(stores, *[(at, 1, False) for at in places])
        post = jnp.concatenate(posts, axis=0)
        counts = jnp.floor_divide(sign * reaches, WIN)
        bottom, top = (lowest, beyond) if sign > 0 else (-beyond, -lowest)
        far = jnp.any((counts < bottom) | (counts >= top))
        own_reach = jnp.stack([sign * each for each in own])
        own_count = jnp.floor_divide(own_reach, WIN)
        turned = jnp.where((own_count < bottom) | (own_count >= top), own_count, 0)
        post = lax.cond(
            far, lambda rows: far_along(rows, turned[:, None, None]), lambda rows: rows, post
        )
        blocks = across(post, outer_pairs, range(bottom, top + 1), sign)
        left = own_reach - turned * WIN
        return stores, [
            between([block[slot] for block in blocks], bottom, left[slot]) for slot in range(2)
        ]

    def forward_sources(block, neighbour, goal):
        return (block, neighbour) if goal <= turn else (neighbour, block)

    def backward_sources(block, neighbour, origin):
        return (neighbour, block) if origin <= turn else (block, neighbour)

    def step_to(goal):
        return 1 if goal <= turn else -1

    skips = {}
    for pair in range(pair_count):
        low, high = 2 * pair, 2 * pair + 1
        stores, z_low = forward(low, sources, skips.get(low), stores)
        neighbour = along(z_low, step_to(high), everyone)
        if pair == half_pairs - 1:
            inner = across(z_low, (pair,), range(-1, 3), 1)
            stores, rows = outer_skips(stores, (Z_AT, LOW_SLOTS + Z_AT), 1)
            neighbour, *rows = together(neighbour, *rows)
            for goal in range(half_pairs + 1, pair_count):
                skips[2 * goal + 1], skips[2 * goal] = rows
        sources = forward_sources(z_low, neighbour, high)
        stores, z_high = forward(high, sources, skips.get(high), stores)
        if pair == half_pairs - 1:
            z_high, *inner = together(z_high, *inner)
            skips[low + 3] = between(inner, -1, start[low + 3] - start[low])
        if pair < pair_count - 1:
            neighbour = hop(z_high, pair, 1, step_to(high + 1))
            sources = forward_sources(hop(z_high, pair, 1, 0), neighbour, high + 1)

    skips = {}
    sources = (z_high, aim, w_head)
    for pair in range(pair_count - 1, -1, -1):
        low, high = 2 * pair, 2 * pair + 1
        stores, gx_high = backward(high, sources, skips.get(high), stores)
        neighbour = along(gx_high, -step_to(high), everyone)
        if pair == half_pairs:
            inner = across(gx_high, (pair,), range(-2, 2), -1)
            stores, rows = outer_skips(stores, (LOW_SLOTS + GX_AT, GX_AT), -1)
            neighbour, *rows = together(neighbour, *rows)
            for goal in outer_encoders:
                skips[2 * goal], skips[2 * goal + 1] = rows
        sources = backward_sources(gx_high, neighbour, high)
        stores, gx_low = backward(low, sources, skips.get(low), stores)
        if pair == half_pairs:
            gx_low, *inner = together(gx_low, *inner)
            skips[high - 3] = between(inner, -2, start[high - 3] - start[high])
        if pair > 0:
            neighbour = hop(gx_low, pair - 1, -1, -step_to(low))
            sources = backward_sources(hop(gx_low, pair - 1, -1, 0), neighbour, low)
        if pair == half_pairs - 1:
            stores, given = picked(stores, (LEFT_AT, LEFT_SLOTS, True))
            *sources, left_other = together(*sources, swap(given[0]))

    stores, given = picked(stores, (RIGHT_AT, RIGHT_SLOTS, True))
    right_other = swap(given[0])
    total = 4 * width + 2 * hidden
    inner = 4
    outer = tok_count // inner
    strip = width // tok_count
    tok_in, tok_out = tok_index % inner, tok_index // inner
    step = width
    parts = pl.pallas_call(
        lambda *refs: weight_kernel(inner, *refs),
        out_shape=[jax.ShapeDtypeStruct((outer, strip, hidden), BF16)] * (3 * inner),
        in_specs=[SMEM] + [HBM] * 3,
        out_specs=[VMEM] * (3 * inner),
        scratch_shapes=[
            pltpu.VMEM((2 * WIN, LEFT_SLOTS * SLOT), BF16),
            pltpu.VMEM((2 * WIN, RIGHT_SLOTS * SLOT), BF16),
            pltpu.VMEM((width, step), BF16),
            pltpu.SemaphoreType.DMA((2 * (LEFT_SLOTS + RIGHT_SLOTS),)),
        ],
        compiler_params=params,
        name="weight_grads",
    )(
        jnp.stack([core_index, tok_in, tok_out]).astype(jnp.int32),
        stores[0],
        left_other,
        right_other,
    )
    early_parts, late_parts, far_parts = [
        parts[group * inner : (group + 1) * inner] for group in range(3)
    ]

    def ring(block, distance, inside):
        route = []
        for tok in range(tok_count):
            far, near = tok // inner, tok % inner
            if inside:
                goal = far * inner + (near + distance) % inner
            else:
                goal = (far + distance) % outer * inner + near
            route.append((tok, goal))
        return lax.ppermute(block, "tok", route)

    def piece(array, index):
        return lax.dynamic_index_in_dim(array, index, 0, False)

    def first_stage(pieces, inside):
        summed = pieces[0].astype(F32)
        for distance in range(1, len(pieces)):
            summed = summed + ring(pieces[distance], distance, inside).astype(F32)
        return summed.astype(BF16)

    def second_stage(summed, position, size, inside):
        result = piece(summed, position).astype(F32)
        for distance in range(1, size):
            sent = piece(summed, (position + distance) % size)
            result = result + ring(sent, distance, inside).astype(F32)
        return result

    early_sums = first_stage(early_parts, True)
    far_sums = first_stage(far_parts, False)
    waiting, *late_parts = together(early_sums, *late_parts)
    late_sums = first_stage(late_parts, True)
    early_sums, far_sums = together(waiting, far_sums)
    early_result = second_stage(early_sums, tok_out, outer, False)
    early_result, late_sums, far_sums = together(early_result, late_sums, far_sums)
    late_result = second_stage(late_sums, tok_out, outer, False)
    far_result = second_stage(far_sums, tok_in, inner, True)
    grad_qkv = early_result[:, : 3 * width][None]
    grad_out = early_result[:, 3 * width :][None]
    grad_up = late_result[None]
    grad_down = far_result[None]
    return (grad_qkv, grad_out, grad_up, grad_down)


def solution(mesh):
    placed = (
        P(None, "tok", None),
        P("section"),
        P("section", None, None),
        P("section", None, None),
        P("section", None, None),
        P("section", None, None),
        P(),
        P(None, "tok", None),
        P(None, "tok", None),
        P(None, "tok"),
        P(None, "tok"),
    )
    return jax.shard_map(
        body,
        mesh=mesh,
        in_specs=placed,
        out_specs=(
            P("section", "tok", None),
            P("section", "tok", None),
            P("section", "tok", None),
            P("section", "tok", None),
        ),
        check_vma=False,
    )
```

```python
import math

import jax
import jax.numpy as jnp
from jax import lax
from jax.experimental import pallas as pl
from jax.experimental.pallas import tpu as pltpu
from jax.sharding import PartitionSpec as P

HEAD_DIM = 32
WIN = 128
LANES = 128
GROUP = LANES // HEAD_DIM

norm_eps = 1e-05
logit_scale = 10.0
floor_share = 0.75
decay_base = 0.8
norm_floor = floor_share * math.sqrt(HEAD_DIM)

F32 = jnp.float32
BF16 = jnp.bfloat16
VMEM_LIMIT = 48 * 1024 * 1024

SLOT = 512
X_AT, QKV_AT, LEFT_AT, RIGHT_AT, Z_AT, GX_AT, LOW_SLOTS = 0, 1, 4, 11, 20, 21, 22
LEFT_SLOTS, RIGHT_SLOTS = 7, 9
Y_AT, U_AT, WIDE_SLOTS = 0, 1, 5
LOW_STORE, WIDE_STORE = 224, 112

NN = (((1,), (0,)), ((), ()))
NT = (((1,), (1,)), ((), ()))
TN = (((0,), (0,)), ((), ()))


def dot(left, right, dims=NN):
    return lax.dot_general(left, right, dims, preferred_element_type=F32)


def norm_parts(values):
    center = values - jnp.mean(values, axis=-1, keepdims=True)
    scale = lax.rsqrt(jnp.mean(center * center, axis=-1, keepdims=True) + norm_eps)
    return center * scale, scale


def norm_back(normed, scale, grad):
    grad_mean = jnp.mean(grad, axis=-1, keepdims=True)
    grad_dot = jnp.mean(grad * normed, axis=-1, keepdims=True)
    return scale * (grad - grad_mean - normed * grad_dot)


def joined(first, second, start):
    both = jnp.concatenate([first.astype(F32), second.astype(F32)], axis=0)
    return pltpu.roll(both, lax.rem(2 * WIN - start, 2 * WIN), 0)[:WIN]


def head_sum(values):
    width = values.shape[1]
    rows = lax.broadcasted_iota(jnp.int32, (LANES, LANES), 0) // HEAD_DIM
    cols = lax.broadcasted_iota(jnp.int32, (LANES, LANES), 1) // HEAD_DIM
    same = (rows == cols).astype(BF16)
    high = values.astype(BF16)
    low = (values - high.astype(F32)).astype(BF16)
    parts = []
    for at in range(0, width, LANES):
        parts.append(dot(high[:, at : at + LANES], same) + dot(low[:, at : at + LANES], same))
    return jnp.concatenate(parts, axis=1)


def spread_heads(rows):
    head = lax.broadcasted_iota(jnp.int32, rows.shape, 1) // HEAD_DIM
    zero = jnp.zeros_like(rows)
    return jnp.concatenate([jnp.where(head == h, rows, zero) for h in range(GROUP)], axis=0)


def gather_heads(stacked):
    head = lax.broadcasted_iota(jnp.int32, (WIN, LANES), 1) // HEAD_DIM
    result = stacked[:WIN]
    for h in range(1, GROUP):
        result = jnp.where(head == h, stacked[h * WIN : (h + 1) * WIN], result)
    return result


def unit_rows(rows):
    length = jnp.sqrt(head_sum(rows * rows))
    inverse = 1.0 / jnp.maximum(length, norm_floor)
    return inverse, length > norm_floor


def gelu_parts(lifted):
    root = math.sqrt(2.0 / math.pi)
    square = lifted * lifted
    bend = jnp.tanh(root * lifted * (1.0 + 0.044715 * square))
    return square, bend, root


def weight_views(ref):
    width = ref.shape[0]
    hidden = (ref.shape[1] - 4 * width) // 2
    views, at = [], 0
    for size in (3 * width, width, hidden, hidden):
        views.append(ref.at[:, pl.ds(at, size)])
        at += size
    return views


def fetch(pairs, own, sems):
    for index, (mine, other, into) in enumerate(pairs):

        @pl.when(own == 1)
        def _():
            pltpu.make_async_copy(mine, into, sems.at[index]).start()

        @pl.when(own == 0)
        def _():
            pltpu.make_async_copy(other, into, sems.at[index]).start()

    def arrived(index):
        pltpu.make_async_copy(pairs[index][0], pairs[index][2], sems.at[index]).wait()

    return arrived


def forward_kernel(mode, section, *refs):
    info_ref = refs[0]

    @pl.when(info_ref[section, 2] == 1)
    def _():
        forward_section(mode, section, *refs)


def forward_section(mode, section, *refs):
    refs = list(refs)
    info_ref, cur_ref, nxt_ref = refs[:3]
    refs = refs[3:]
    skip_ref = refs.pop(0) if mode == "skip" else None
    mine, other = weight_views(refs[0]), weight_views(refs[1])
    low_store, wide_store, z_ref = refs[4:7]
    held = refs[7:11]
    x_ref, qkv_ref, left_ref, y_ref, u_ref, sems, out_sems = refs[11:]
    arrived = fetch(list(zip(mine, other, held)), info_ref[section, 1], sems)
    w_qkv, w_out, w_up, w_down = held
    low_base, wide_base = section % 2 * LOW_SLOTS, section % 2 * WIDE_SLOTS
    out_copies = []

    def keep(room, store, at):
        goal = store.at[pl.ds(at, room.shape[0])]
        copy = pltpu.make_async_copy(room, goal, out_sems.at[len(out_copies)])
        copy.start()
        out_copies.append(copy)

    x = joined(cur_ref[...], nxt_ref[...], info_ref[section, 0])
    if mode == "skip":
        x = (x + skip_ref[...].astype(F32)).astype(BF16).astype(F32)
    if mode == "double":
        x = x + x
    x_ref[0] = x.astype(BF16)
    keep(x_ref, low_store, low_base + X_AT)
    n1 = norm_parts(x)[0].astype(BF16)
    left_ref[0] = n1
    arrived(0)
    q, k, v = [dot(n1, w_qkv[:, at : at + SLOT]).astype(BF16) for at in (0, SLOT, 2 * SLOT)]
    qkv_ref[0] = q
    qkv_ref[1] = k
    qkv_ref[2] = v
    keep(qkv_ref, low_store, low_base + QKV_AT)
    q = q.astype(F32)
    k = k.astype(F32)
    qh = (q * (logit_scale * unit_rows(q)[0])).astype(BF16)
    kh = (k * unit_rows(k)[0]).astype(BF16)
    ones = jnp.ones((WIN, LANES), BF16)
    attended = []
    for at in range(0, SLOT, LANES):
        scores = dot(spread_heads(qh[:, at : at + LANES]), kh[:, at : at + LANES], NT)
        weights = jnp.exp(scores).astype(BF16)
        mixed = dot(weights, jnp.concatenate([v[:, at : at + LANES], ones], axis=1))
        attended.append(gather_heads(mixed[:, :LANES] / mixed[:, LANES:]))
    att = jnp.concatenate(attended, axis=1).astype(BF16)
    left_ref[1] = att
    arrived(1)
    y = x + dot(att, w_out[...])
    y_ref[0] = y
    keep(y_ref, wide_store, wide_base + Y_AT)
    n2 = norm_parts(y)[0].astype(BF16)
    left_ref[2] = n2
    arrived(2)
    for index in range(LEFT_SLOTS - 3):
        u = dot(n2, w_up[:, index * SLOT : (index + 1) * SLOT])
        u_ref[index] = u
        bend = gelu_parts(u)[1]
        left_ref[3 + index] = (0.5 * u * (1.0 + bend)).astype(BF16)
    keep(u_ref, wide_store, wide_base + U_AT)
    keep(left_ref, low_store, low_base + LEFT_AT)
    arrived(3)
    z = y
    for index in range(LEFT_SLOTS - 3):
        z = z + dot(left_ref[3 + index], w_down[:, index * SLOT : (index + 1) * SLOT], NT)
    z_ref[...] = z.astype(BF16)
    posted = pltpu.make_async_copy(z_ref, low_store.at[low_base + Z_AT], out_sems.at[5])
    posted.start()
    for copy in out_copies + [posted]:
        copy.wait()


def backward_kernel(mode, last, section, *refs):
    info_ref = refs[0]

    @pl.when(info_ref[section, 2] == 1)
    def _():
        backward_section(mode, last, section, *refs)


def backward_section(mode, last, section, *refs):
    refs = list(refs)
    info_ref = refs.pop(0)
    if mode == "head":
        z_ref, aim_ref, head_ref = refs[:3]
        refs = refs[3:]
    else:
        cur_ref, prv_ref = refs[:2]
        refs = refs[2:]
    skip_ref = refs.pop(0) if mode == "skip" else None
    mine, other = weight_views(refs[0]), weight_views(refs[1])
    low_store, wide_store, gx_ref = refs[4:7]
    held = refs[7:11]
    x_ref, qkv_ref, right_ref, y_ref, u_ref, sems, in_sems, out_sem = refs[11:]
    low_base, wide_base = section % 2 * LOW_SLOTS, section % 2 * WIDE_SLOTS
    in_copies = [
        pltpu.make_async_copy(store.at[pl.ds(at, room.shape[0])], room, in_sems.at[index])
        for index, (room, store, at) in enumerate(
            [
                (x_ref, low_store, low_base + X_AT),
                (y_ref, wide_store, wide_base + Y_AT),
                (u_ref, wide_store, wide_base + U_AT),
                (qkv_ref, low_store, low_base + QKV_AT),
            ]
        )
    ]
    pairs = list(zip(mine, other, held))
    arrived = fetch(pairs[::-1], info_ref[section, 1], sems)
    for index in (2, 1, 3, 0):
        in_copies[index].start()
    w_qkv, w_out, w_up, w_down = held
    hidden_slots = u_ref.shape[0]

    if mode == "head":
        normed, scale = norm_parts(z_ref[...].astype(F32))
        channels = head_ref.shape[1]
        predicted = dot(normed.astype(BF16), head_ref[...])
        target = aim_ref[:, :channels].astype(F32)
        bucket = aim_ref[:, channels:].astype(F32)
        decay = jnp.exp(bucket * math.log(decay_base))
        loss_scale = 1.0 / math.sqrt(2 * 16 * WIN)
        grad_pred = (decay * (predicted - target) * loss_scale).astype(BF16)
        dz = norm_back(normed, scale, dot(grad_pred, head_ref[...], NT))
    else:
        dz = joined(prv_ref[...], cur_ref[...], WIN - info_ref[section, 3])
        if mode == "skip":
            dz = dz + skip_ref[...].astype(F32)
        if mode == "double":
            dz = dz + dz
    g_m = dz.astype(BF16)
    right_ref[4 + hidden_slots] = g_m
    arrived(0)
    in_copies[2].wait()
    for index in range(hidden_slots):
        dh = dot(g_m, w_down[:, index * SLOT : (index + 1) * SLOT])
        u = u_ref[index]
        square, bend, root = gelu_parts(u)
        slope = 0.5 * (1.0 + bend) + (0.5 * root) * u * (1.0 - bend * bend) * (
            1.0 + 3 * 0.044715 * square
        )
        right_ref[4 + index] = (slope * dh).astype(BF16)
    arrived(1)
    dn2 = dot(right_ref[4], w_up[:, :SLOT], NT)
    for index in range(1, hidden_slots):
        dn2 = dn2 + dot(right_ref[4 + index], w_up[:, index * SLOT : (index + 1) * SLOT], NT)
    in_copies[1].wait()
    normed, scale = norm_parts(y_ref[0])
    dy = dz + norm_back(normed, scale, dn2)
    g_a = dy.astype(BF16)
    right_ref[3] = g_a
    arrived(2)
    da = dot(g_a, w_out[...], NT).astype(BF16)

    in_copies[3].wait()
    q = qkv_ref[0].astype(F32)
    k = qkv_ref[1].astype(F32)
    q_inv, q_free = unit_rows(q)
    k_inv, k_free = unit_rows(k)
    qu = q * q_inv
    ku = k * k_inv
    qh = (logit_scale * qu).astype(BF16)
    kh = ku.astype(BF16)
    ones = jnp.ones((WIN, LANES), BF16)
    dq_parts, dk_parts = [], []
    for at in range(0, SLOT, LANES):
        kg = kh[:, at : at + LANES]
        vg = qkv_ref[2, :, at : at + LANES]
        queries = spread_heads(qh[:, at : at + LANES])
        weights = jnp.exp(dot(queries, kg, NT))
        probs = weights / dot(weights.astype(BF16), ones)
        probs_low = probs.astype(BF16)
        grads = spread_heads(da[:, at : at + LANES])
        dp = dot(grads, vg, NT)
        ds = (probs * (dp - dot((probs * dp).astype(BF16), ones))).astype(BF16)
        right_ref[2, :, at : at + LANES] = dot(probs_low, grads, TN).astype(BF16)
        dq_parts.append(gather_heads(dot(ds, kg)))
        dk_parts.append(dot(ds, queries, TN))
    dqh = logit_scale * jnp.concatenate(dq_parts, axis=1)
    dkh = jnp.concatenate(dk_parts, axis=1)
    dq = q_inv * (dqh - jnp.where(q_free, qu * head_sum(qu * dqh), 0.0))
    dk = k_inv * (dkh - jnp.where(k_free, ku * head_sum(ku * dkh), 0.0))
    right_ref[0] = dq.astype(BF16)
    right_ref[1] = dk.astype(BF16)
    right_goal = low_store.at[pl.ds(low_base + RIGHT_AT, RIGHT_SLOTS)]
    out_copy = pltpu.make_async_copy(right_ref, right_goal, out_sem.at[0])
    out_copy.start()
    arrived(3)
    in_copies[0].wait()
    if last:
        gx_ref[...] = g_a
    else:
        dn1 = dot(right_ref[0], w_qkv[:, :SLOT], NT)
        for index in (1, 2):
            dn1 = dn1 + dot(right_ref[index], w_qkv[:, index * SLOT : (index + 1) * SLOT], NT)
        normed, scale = norm_parts(x_ref[0].astype(F32))
        gx_ref[...] = (dy + norm_back(normed, scale, dn1)).astype(BF16)
    posted = pltpu.make_async_copy(gx_ref, low_store.at[low_base + GX_AT], out_sem.at[1])
    posted.start()
    out_copy.wait()
    posted.wait()


def pick_kernel(ranges, *refs):
    core_ref, store_ref = refs[:2]
    outs, sems = refs[3:-1], refs[-1]
    copies = []
    for index, (at, count, given) in enumerate(ranges):
        base = at + (1 - core_ref[0]) * LOW_SLOTS if given else at
        source = store_ref.at[pl.ds(base, count)]
        copies.append(pltpu.make_async_copy(source, outs[index], sems.at[index]))
        copies[-1].start()
    for copy in copies:
        copy.wait()


def weight_kernel(inner, *refs):
    info_ref, store_ref = refs[:2]
    received = refs[2:4]
    near_refs, far_refs = refs[4 : 4 + inner], refs[4 + inner : 4 + 2 * inner]
    left, right, room, sems = refs[4 + 2 * inner :]
    copies = []
    for into, at, count, got in ((left, LEFT_AT, LEFT_SLOTS, 0), (right, RIGHT_AT, RIGHT_SLOTS, 1)):
        for index in range(count):
            columns = pl.ds(index * SLOT, SLOT)
            for part in range(2):
                goal = into.at[pl.ds(part * WIN, WIN), columns]
                sem = sems.at[len(copies)]
                if part == 0:
                    source = store_ref.at[info_ref[0] * LOW_SLOTS + at + index]
                else:
                    source = received[got].at[index]
                copies.append(pltpu.make_async_copy(source, goal, sem))
                copies[-1].start()
    for copy in copies:
        copy.wait()
    width, step = room.shape
    hidden = right.shape[1] - 5 * width
    total = 4 * width + 2 * hidden
    outer = near_refs[0].shape[0]
    strip = near_refs[0].shape[1]
    split = near_refs[0].shape[2]
    for at in range(0, total, step):
        if at < 3 * width:
            first, second = left[:, :width], right[:, at : at + step]
        elif at < 4 * width:
            first, second = left[:, width : 2 * width], right[:, at : at + step]
        elif at < 4 * width + hidden:
            first, second = left[:, 2 * width : 3 * width], right[:, at : at + step]
        else:
            start = 3 * width + at - 4 * width - hidden
            first, second = right[:, 4 * width + hidden :], left[:, start : start + step]
        room[...] = dot(first, second, TN).astype(BF16)
        for distance in range(inner):
            if at < split:
                column = lax.rem(info_ref[1] + distance, inner)
            else:
                column = lax.rem(info_ref[2] + distance, outer)
            for line in range(outer):
                if at < split:
                    owner = line * inner + column
                    near_refs[distance][line, :, at : at + step] = room[
                        pl.ds(owner * strip, strip), :
                    ]
                else:
                    owner = column * inner + line
                    far_refs[distance][line, :, at - split : at - split + step] = room[
                        pl.ds(owner * strip, strip), :
                    ]


VMEM = pl.BlockSpec(memory_space=pltpu.VMEM)
SMEM = pl.BlockSpec(memory_space=pltpu.SMEM)
HBM = pl.BlockSpec(memory_space=pltpu.HBM)


def body(tokens, offsets, w_qkv, w_out, w_up, w_down, w_head, era5t, era5, flags, buckets):
    section_count = lax.axis_size("section")
    tok_count = lax.axis_size("tok")
    pair_count = section_count // 2
    half_pairs = pair_count // 2
    section_index = lax.axis_index("section")
    tok_index = lax.axis_index("tok")
    pair_index = section_index // 2
    core_index = section_index % 2
    micro_count, row_count, width = tokens.shape
    hidden = w_up.shape[2]
    mine = jnp.concatenate([w_qkv[0], w_out[0], w_up[0], w_down[0]], axis=1)

    def place(section, tok):
        return section * tok_count + tok % tok_count

    def moved(block, route):
        return lax.ppermute(block, ("section", "tok"), route)

    def hop(block, low_pair, step, tok_shift):
        middle = half_pairs - 1
        route = []
        for pair in range(pair_count - 1):
            if (pair > middle) - (pair < middle) == (low_pair > middle) - (low_pair < middle):
                for core in range(2):
                    for tok in range(tok_count):
                        low, high = 2 * pair + core, 2 * pair + 2 + core
                        origin, goal = (low, high) if step > 0 else (high, low)
                        route.append((place(origin, tok + tok_shift), place(goal, tok)))
        return moved(block, sorted(route))

    def along(block, tok_shift, sections):
        route = []
        for section in sections:
            for tok in range(tok_count):
                route.append((place(section, tok + tok_shift), place(section, tok)))
        return moved(block, route)

    def mirror(block, pairs):
        route = []
        for one in pairs:
            for goal in (pair_count - 1 - one,):
                for core in range(2):
                    for tok in range(tok_count):
                        origin = 2 * (pair_count - 1 - goal) + core
                        route.append((place(origin, tok), place(2 * goal + core, tok)))
        return moved(block, sorted(route))

    def swap(block):
        route = [
            (place(section, tok), place(section ^ 1, tok))
            for section in range(section_count)
            for tok in range(tok_count)
        ]
        return moved(block, route)

    def inner_hops(block, pair, sign):
        goal = pair_count - 1 - pair
        return [
            moved(
                block,
                sorted(
                    (place(2 * pair + core, tok + sign * index), place(2 * goal + core, tok))
                    for core in range(2)
                    for tok in range(tok_count)
                ),
            )
            for index in range(4)
        ]

    everyone = range(section_count)
    last_encoder = section_count // 2 - 1
    encoders = range(last_encoder - 1)
    decoders = range(last_encoder + 3, section_count)

    def far_along(block, blocks, limit, sign, sections):
        bit = 1
        while bit <= limit:
            inner = sections[:2] if sections[0] > 0 else sections[-2:]
            taking = [one for one in sections if bit < tok_count // 2 or one not in inner]
            shifted = along(block, sign * bit, taking)
            block = jnp.where((blocks // bit) % 2 == 1, shifted, block)
            bit *= 2
        return block

    def together(*arrays):
        return lax.optimization_barrier(arrays)

    table = lax.all_gather(offsets, "section").reshape(section_count)
    order = jnp.arange(section_count)
    before = jnp.where(order == 0, 0, jnp.roll(table, 1))
    shifts = (table - before + WIN) % WIN
    start = jnp.sum(jnp.where(order[:, None] >= order[None, :], shifts[None, :], 0), axis=1)

    other = swap(mine)

    info = jnp.stack(
        [
            shifts,
            (core_index == order % 2).astype(jnp.int32),
            (pair_index == order // 2).astype(jnp.int32),
            jnp.roll(shifts, -1),
        ],
        axis=1,
    ).astype(jnp.int32)

    weight_rooms = [
        pltpu.VMEM(weight.shape[1:], BF16) for weight in (w_qkv, w_out, w_up, w_down)
    ]
    weight_sems = pltpu.SemaphoreType.DMA((4,))
    rows_bf = jax.ShapeDtypeStruct((WIN, width), BF16)
    store_shapes = (
        jax.ShapeDtypeStruct((LOW_STORE, WIN, SLOT), BF16),
        jax.ShapeDtypeStruct((WIDE_STORE, WIN, SLOT), F32),
    )
    channels = era5.shape[2]
    hidden_slots = hidden // SLOT

    def room(count, dtype):
        return pltpu.VMEM((count, WIN, SLOT), dtype)

    params = pltpu.CompilerParams(vmem_limit_bytes=VMEM_LIMIT)

    def section_call(kernel, name, inputs, stores, rooms, sems):
        inputs = [info, *inputs]
        first = len(inputs) + 2
        result = pl.pallas_call(
            kernel,
            out_shape=store_shapes + (rows_bf,),
            in_specs=[SMEM] + [VMEM] * (len(inputs) - 1) + [HBM] * 4,
            out_specs=(HBM, HBM, VMEM),
            input_output_aliases={first: 0, first + 1: 1},
            scratch_shapes=weight_rooms
            + rooms
            + [room(1, F32), room(hidden_slots, F32), weight_sems]
            + [pltpu.SemaphoreType.DMA((count,)) for count in sems],
            compiler_params=params,
            name=name,
        )(*inputs, mine, other, *stores)
        return tuple(result[:2]), result[2]

    def forward(section, cur, nxt, skip, stores):
        if section < section_count // 2:
            mode = "plain"
        else:
            mode = "double" if section == section_count // 2 else "skip"
        return section_call(
            lambda *refs: forward_kernel(mode, section, *refs),
            "forward_" + mode,
            [cur, nxt] + ([skip] if mode == "skip" else []),
            stores,
            [room(1, BF16), room(3, BF16), room(LEFT_SLOTS, BF16)],
            (6,),
        )

    def backward(section, sources, skip, stores):
        if section == section_count - 1:
            mode = "head"
        elif section >= section_count // 2:
            mode = "plain"
        else:
            mode = "double" if section == section_count // 2 - 1 else "skip"
        return section_call(
            lambda *refs: backward_kernel(mode, section == 0, section, *refs),
            "backward_" + mode,
            [*sources] + ([skip] if mode == "skip" else []),
            stores,
            [room(1, BF16), room(3, BF16), room(RIGHT_SLOTS, BF16)],
            (4, 2),
        )

    core_scalar = core_index[None].astype(jnp.int32)

    def picked(stores, *ranges):
        result = pl.pallas_call(
            lambda *refs: pick_kernel(ranges, *refs),
            out_shape=(store_shapes[0],)
            + tuple(jax.ShapeDtypeStruct((count, WIN, SLOT), BF16) for _, count, _ in ranges),
            in_specs=[SMEM, HBM],
            out_specs=(HBM,) + (VMEM,) * len(ranges),
            input_output_aliases={1: 0},
            scratch_shapes=[pltpu.SemaphoreType.DMA((len(ranges),))],
            name="pick",
        )(core_scalar, stores[0])
        return (result[0], stores[1]), result[1:]

    def unwritten():
        return pl.pallas_call(
            lambda *refs: None,
            out_shape=store_shapes,
            out_specs=(HBM,) * 2,
            name="unwritten",
        )()

    cur = lax.dynamic_index_in_dim(tokens, core_index, 0, False)
    nxt = along(cur, 1, everyone)
    stores = unwritten()
    chosen = jnp.repeat(
        lax.dynamic_index_in_dim(flags, core_index, 0, False), row_count // flags.shape[1]
    )
    target = jnp.where(
        (chosen == 1)[:, None],
        lax.dynamic_index_in_dim(era5t, core_index, 0, False),
        lax.dynamic_index_in_dim(era5, core_index, 0, False),
    )
    bucket = lax.dynamic_index_in_dim(buckets, core_index, 0, False).astype(BF16)
    bucket = jnp.broadcast_to(bucket[:, None], target.shape)
    aim_here = jnp.stack([target, bucket])

    low_reach = start[section_count - 1 - 2 * pair_index] - start[2 * pair_index]
    high_reach = start[section_count - 2 - 2 * pair_index] - start[2 * pair_index + 1]
    reaches = [jnp.abs(low_reach), jnp.abs(high_reach)]
    reaches_seen = [
        jnp.where(pair_index < half_pairs, reaches[slot], reaches[1 - slot]) for slot in range(2)
    ]
    target_reach = start[section_count - 1]

    def cut(first, second, at):
        return lax.dynamic_slice_in_dim(jnp.concatenate([first, second], axis=0), at, WIN, 0)

    def long_shift(blocks, counts, limit, sign, sections):
        near = far_along(blocks, counts, limit, sign, sections)
        return near, along(near, sign, sections)

    def near_and_beside(blocks, count):
        near, beside = blocks[0], blocks[1]
        for index in range(1, len(blocks) - 1):
            near = jnp.where(count == index, blocks[index], near)
            beside = jnp.where(count == index, blocks[index + 1], beside)
        return near, beside

    def outer_skips(stores, first, second, limit, sign, sections, with_aim):
        stores, posts = picked(stores, (first, 1, False), (second, 1, False))
        post = jnp.concatenate(posts, axis=0)
        counts = [jnp.full((1, 1, width), each // WIN) for each in reaches_seen]
        if with_aim:
            post = jnp.concatenate([post, aim_here], axis=2)
            extra = jnp.full((1, 1, channels), target_reach // WIN)
            counts = [jnp.concatenate([count, extra], axis=2) for count in counts]
        near, beside = long_shift(
            mirror(post, outer_encoders if sign > 0 else outer_decoders),
            jnp.concatenate(counts, axis=0),
            limit,
            sign,
            sections,
        )
        rows = []
        for slot in range(2):
            here, there = near[slot, :, :width], beside[slot, :, :width]
            left = reaches_seen[slot] % WIN
            rows.append(cut(here, there, left) if sign > 0 else cut(there, here, WIN - left))
        if with_aim:
            aims = [
                cut(near[slot, :, width:], beside[slot, :, width:], target_reach % WIN)
                for slot in range(2)
            ]
            rows.append(jnp.concatenate(aims, axis=1))
        return stores, rows

    outer_encoders = range(half_pairs - 1)
    outer_decoders = range(half_pairs + 1, pair_count)
    skips = {}
    aim = None
    for pair in range(pair_count):
        low, high = 2 * pair, 2 * pair + 1
        stores, z_low = forward(low, cur, nxt, skips.get(low), stores)
        nxt = along(z_low, 1, everyone)
        if pair == half_pairs - 1:
            inner = inner_hops(z_low, pair, 1)
        stores, z_high = forward(high, z_low, nxt, skips.get(high), stores)
        if pair == half_pairs - 1:
            z_high, *inner = together(z_high, *inner)
        if pair < pair_count - 1:
            nxt = hop(z_high, pair, 1, 1)
            cur = hop(z_high, pair, 1, 0)
        if pair == half_pairs - 2:
            stores, rows = outer_skips(
                stores, Z_AT, LOW_SLOTS + Z_AT, tok_count - 1, 1, decoders, True
            )
            cur, nxt, *rows = together(cur, nxt, *rows)
            aim = rows[2]
            for goal in range(half_pairs + 1, pair_count):
                skips[2 * goal + 1], skips[2 * goal] = rows[:2]
        if pair == half_pairs - 1:
            reach = start[low + 3] - start[low]
            near, beside = near_and_beside(inner, reach // WIN)
            skips[low + 3] = cut(near, beside, reach % WIN)

    skips = {}
    sources = (z_high, aim, w_head)
    for pair in range(pair_count - 1, -1, -1):
        low, high = 2 * pair, 2 * pair + 1
        stores, gx_high = backward(high, sources, skips.get(high), stores)
        prv = along(gx_high, -1, everyone)
        if pair == half_pairs:
            inner = inner_hops(gx_high, pair, -1)
        sources = (gx_high, prv)
        stores, gx_low = backward(low, sources, skips.get(low), stores)
        if pair == half_pairs:
            gx_low, *inner = together(gx_low, *inner)
        if pair > 0:
            prv = hop(gx_low, pair - 1, -1, -1)
            cur = hop(gx_low, pair - 1, -1, 0)
            sources = (cur, prv)
        if pair == half_pairs + 1:
            stores, rows = outer_skips(
                stores, LOW_SLOTS + GX_AT, GX_AT, tok_count - 2, -1, encoders, False
            )
            cur, prv, *rows = together(cur, prv, *rows)
            sources = (cur, prv)
            for goal in range(half_pairs - 1):
                skips[2 * goal], skips[2 * goal + 1] = rows
        if pair == half_pairs:
            reach = start[high] - start[high - 3]
            near, beside = near_and_beside(inner, reach // WIN)
            skips[high - 3] = cut(beside, near, WIN - reach % WIN)
        if pair == half_pairs - 1:
            stores, given = picked(stores, (LEFT_AT, LEFT_SLOTS, True))
            cur, prv, left_other = together(cur, prv, swap(given[0]))
            sources = (cur, prv)

    stores, given = picked(stores, (RIGHT_AT, RIGHT_SLOTS, True))
    right_other = swap(given[0])
    total = 4 * width + 2 * hidden
    inner = 4
    outer = tok_count // inner
    strip = width // tok_count
    split = 4 * width + hidden
    tok_in, tok_out = tok_index % inner, tok_index // inner
    step = width
    parts = pl.pallas_call(
        lambda *refs: weight_kernel(inner, *refs),
        out_shape=[jax.ShapeDtypeStruct((outer, strip, split), BF16)] * inner
        + [jax.ShapeDtypeStruct((inner, strip, total - split), BF16)] * outer,
        in_specs=[SMEM] + [HBM] * 3,
        out_specs=[VMEM] * (inner + outer),
        scratch_shapes=[
            pltpu.VMEM((2 * WIN, LEFT_SLOTS * SLOT), BF16),
            pltpu.VMEM((2 * WIN, RIGHT_SLOTS * SLOT), BF16),
            pltpu.VMEM((width, step), BF16),
            pltpu.SemaphoreType.DMA((2 * (LEFT_SLOTS + RIGHT_SLOTS),)),
        ],
        compiler_params=params,
        name="weight_grads",
    )(
        jnp.stack([core_index, tok_in, tok_out]).astype(jnp.int32),
        stores[0],
        left_other,
        right_other,
    )
    near_parts, far_parts = parts[:inner], parts[inner:]

    def ring(block, distance, inside):
        route = []
        for tok in range(tok_count):
            far, near = tok // inner, tok % inner
            if inside:
                goal = far * inner + (near + distance) % inner
            else:
                goal = (far + distance) % outer * inner + near
            route.append((tok, goal))
        return lax.ppermute(block, "tok", route)

    def piece(array, index):
        return lax.dynamic_index_in_dim(array, index, 0, False)

    def first_stage(pieces, inside):
        summed = pieces[0].astype(F32)
        for distance in range(1, len(pieces)):
            summed = summed + ring(pieces[distance], distance, inside).astype(F32)
        return summed.astype(BF16)

    def second_stage(summed, position, size, inside):
        result = piece(summed, position).astype(F32)
        for distance in range(1, size):
            sent = piece(summed, (position + distance) % size)
            result = result + ring(sent, distance, inside).astype(F32)
        return result

    near_sums = first_stage(near_parts, True)
    far_sums = first_stage(far_parts, False)
    near_sums, far_sums = together(near_sums, far_sums)
    near_result = second_stage(near_sums, tok_out, outer, False)
    far_result = second_stage(far_sums, tok_in, inner, True)
    grad_qkv = near_result[:, : 3 * width][None]
    grad_out = near_result[:, 3 * width : 4 * width][None]
    grad_up = near_result[:, 4 * width :][None]
    grad_down = far_result[None]
    return (grad_qkv, grad_out, grad_up, grad_down)


def solution(mesh):
    placed = (
        P(None, "tok", None),
        P("section"),
        P("section", None, None),
        P("section", None, None),
        P("section", None, None),
        P("section", None, None),
        P(),
        P(None, "tok", None),
        P(None, "tok", None),
        P(None, "tok"),
        P(None, "tok"),
    )
    return jax.shard_map(
        body,
        mesh=mesh,
        in_specs=placed,
        out_specs=(
            P("section", "tok", None),
            P("section", "tok", None),
            P("section", "tok", None),
            P("section", "tok", None),
        ),
        check_vma=False,
    )
```

```python
import math

import jax
import jax.numpy as jnp
from jax import lax
from jax.experimental import pallas as pl
from jax.experimental.pallas import tpu as pltpu
from jax.sharding import PartitionSpec as P

HEAD_DIM = 32
WIN = 128
LANES = 128
GROUP = LANES // HEAD_DIM

norm_eps = 1e-05
logit_scale = 10.0
floor_share = 0.75
decay_base = 0.8
norm_floor = floor_share * math.sqrt(HEAD_DIM)

F32 = jnp.float32
BF16 = jnp.bfloat16
VMEM_LIMIT = 48 * 1024 * 1024

SLOT = 512
X_AT, QKV_AT, LEFT_AT, RIGHT_AT, Z_AT, GX_AT, LOW_SLOTS = 0, 1, 4, 11, 20, 21, 22
LEFT_SLOTS, RIGHT_SLOTS = 7, 9
Y_AT, U_AT, WIDE_SLOTS = 0, 1, 5
LOW_STORE, WIDE_STORE = 224, 112

NN = (((1,), (0,)), ((), ()))
NT = (((1,), (1,)), ((), ()))
TN = (((0,), (0,)), ((), ()))


def dot(left, right, dims=NN):
    return lax.dot_general(left, right, dims, preferred_element_type=F32)


def norm_parts(values):
    center = values - jnp.mean(values, axis=-1, keepdims=True)
    scale = lax.rsqrt(jnp.mean(center * center, axis=-1, keepdims=True) + norm_eps)
    return center * scale, scale


def norm_back(normed, scale, grad):
    grad_mean = jnp.mean(grad, axis=-1, keepdims=True)
    grad_dot = jnp.mean(grad * normed, axis=-1, keepdims=True)
    return scale * (grad - grad_mean - normed * grad_dot)


def joined(first, second, start):
    both = jnp.concatenate([first.astype(F32), second.astype(F32)], axis=0)
    return pltpu.roll(both, lax.rem(2 * WIN - start, 2 * WIN), 0)[:WIN]


def head_sum(values):
    width = values.shape[1]
    rows = lax.broadcasted_iota(jnp.int32, (LANES, LANES), 0) // HEAD_DIM
    cols = lax.broadcasted_iota(jnp.int32, (LANES, LANES), 1) // HEAD_DIM
    same = (rows == cols).astype(BF16)
    high = values.astype(BF16)
    low = (values - high.astype(F32)).astype(BF16)
    parts = []
    for at in range(0, width, LANES):
        parts.append(dot(high[:, at : at + LANES], same) + dot(low[:, at : at + LANES], same))
    return jnp.concatenate(parts, axis=1)


def spread_heads(rows):
    head = lax.broadcasted_iota(jnp.int32, rows.shape, 1) // HEAD_DIM
    zero = jnp.zeros_like(rows)
    return jnp.concatenate([jnp.where(head == h, rows, zero) for h in range(GROUP)], axis=0)


def gather_heads(stacked):
    head = lax.broadcasted_iota(jnp.int32, (WIN, LANES), 1) // HEAD_DIM
    result = stacked[:WIN]
    for h in range(1, GROUP):
        result = jnp.where(head == h, stacked[h * WIN : (h + 1) * WIN], result)
    return result


def unit_rows(rows):
    length = jnp.sqrt(head_sum(rows * rows))
    inverse = 1.0 / jnp.maximum(length, norm_floor)
    return inverse, length > norm_floor


def gelu_parts(lifted):
    root = math.sqrt(2.0 / math.pi)
    square = lifted * lifted
    bend = jnp.tanh(root * lifted * (1.0 + 0.044715 * square))
    return square, bend, root


def weight_views(ref):
    width = ref.shape[0]
    hidden = (ref.shape[1] - 4 * width) // 2
    views, at = [], 0
    for size in (3 * width, width, hidden, hidden):
        views.append(ref.at[:, pl.ds(at, size)])
        at += size
    return views


def fetch(pairs, own, sems):
    for index, (mine, other, into) in enumerate(pairs):

        @pl.when(own == 1)
        def _():
            pltpu.make_async_copy(mine, into, sems.at[index]).start()

        @pl.when(own == 0)
        def _():
            pltpu.make_async_copy(other, into, sems.at[index]).start()

    def arrived(index):
        pltpu.make_async_copy(pairs[index][0], pairs[index][2], sems.at[index]).wait()

    return arrived


def forward_kernel(mode, section, *refs):
    info_ref = refs[0]

    @pl.when(info_ref[section, 2] == 1)
    def _():
        forward_section(mode, section, *refs)


def forward_section(mode, section, *refs):
    refs = list(refs)
    info_ref, cur_ref, nxt_ref = refs[:3]
    refs = refs[3:]
    skip_ref = refs.pop(0) if mode == "skip" else None
    mine, other = weight_views(refs[0]), weight_views(refs[1])
    low_store, wide_store, z_ref = refs[4:7]
    held = refs[7:11]
    x_ref, qkv_ref, left_ref, y_ref, u_ref, sems, out_sems = refs[11:]
    arrived = fetch(list(zip(mine, other, held)), info_ref[section, 1], sems)
    w_qkv, w_out, w_up, w_down = held
    low_base, wide_base = section % 2 * LOW_SLOTS, section % 2 * WIDE_SLOTS
    out_copies = []

    def keep(room, store, at):
        goal = store.at[pl.ds(at, room.shape[0])]
        copy = pltpu.make_async_copy(room, goal, out_sems.at[len(out_copies)])
        copy.start()
        out_copies.append(copy)

    x = joined(cur_ref[...], nxt_ref[...], info_ref[section, 0])
    if mode == "skip":
        x = (x + skip_ref[...].astype(F32)).astype(BF16).astype(F32)
    if mode == "double":
        x = x + x
    x_ref[0] = x.astype(BF16)
    keep(x_ref, low_store, low_base + X_AT)
    n1 = norm_parts(x)[0].astype(BF16)
    left_ref[0] = n1
    arrived(0)
    q, k, v = [dot(n1, w_qkv[:, at : at + SLOT]).astype(BF16) for at in (0, SLOT, 2 * SLOT)]
    qkv_ref[0] = q
    qkv_ref[1] = k
    qkv_ref[2] = v
    keep(qkv_ref, low_store, low_base + QKV_AT)
    q = q.astype(F32)
    k = k.astype(F32)
    qh = (q * (logit_scale * unit_rows(q)[0])).astype(BF16)
    kh = (k * unit_rows(k)[0]).astype(BF16)
    ones = jnp.ones((WIN, LANES), BF16)
    attended = []
    for at in range(0, SLOT, LANES):
        scores = dot(spread_heads(qh[:, at : at + LANES]), kh[:, at : at + LANES], NT)
        weights = jnp.exp(scores).astype(BF16)
        mixed = dot(weights, jnp.concatenate([v[:, at : at + LANES], ones], axis=1))
        attended.append(gather_heads(mixed[:, :LANES] / mixed[:, LANES:]))
    att = jnp.concatenate(attended, axis=1).astype(BF16)
    left_ref[1] = att
    arrived(1)
    y = x + dot(att, w_out[...])
    y_ref[0] = y
    keep(y_ref, wide_store, wide_base + Y_AT)
    n2 = norm_parts(y)[0].astype(BF16)
    left_ref[2] = n2
    arrived(2)
    for index in range(LEFT_SLOTS - 3):
        u = dot(n2, w_up[:, index * SLOT : (index + 1) * SLOT])
        u_ref[index] = u
        bend = gelu_parts(u)[1]
        left_ref[3 + index] = (0.5 * u * (1.0 + bend)).astype(BF16)
    keep(u_ref, wide_store, wide_base + U_AT)
    keep(left_ref, low_store, low_base + LEFT_AT)
    arrived(3)
    z = y
    for index in range(LEFT_SLOTS - 3):
        z = z + dot(left_ref[3 + index], w_down[:, index * SLOT : (index + 1) * SLOT], NT)
    z_ref[...] = z.astype(BF16)
    posted = pltpu.make_async_copy(z_ref, low_store.at[low_base + Z_AT], out_sems.at[5])
    posted.start()
    for copy in out_copies + [posted]:
        copy.wait()


def backward_kernel(mode, last, section, *refs):
    info_ref = refs[0]

    @pl.when(info_ref[section, 2] == 1)
    def _():
        backward_section(mode, last, section, *refs)


def backward_section(mode, last, section, *refs):
    refs = list(refs)
    info_ref = refs.pop(0)
    if mode == "head":
        z_ref, aim_ref, head_ref = refs[:3]
        refs = refs[3:]
    else:
        cur_ref, prv_ref = refs[:2]
        refs = refs[2:]
    skip_ref = refs.pop(0) if mode == "skip" else None
    mine, other = weight_views(refs[0]), weight_views(refs[1])
    low_store, wide_store, gx_ref = refs[4:7]
    held = refs[7:11]
    x_ref, qkv_ref, right_ref, y_ref, u_ref, sems, in_sems, out_sem = refs[11:]
    low_base, wide_base = section % 2 * LOW_SLOTS, section % 2 * WIDE_SLOTS
    in_copies = [
        pltpu.make_async_copy(store.at[pl.ds(at, room.shape[0])], room, in_sems.at[index])
        for index, (room, store, at) in enumerate(
            [
                (x_ref, low_store, low_base + X_AT),
                (y_ref, wide_store, wide_base + Y_AT),
                (u_ref, wide_store, wide_base + U_AT),
                (qkv_ref, low_store, low_base + QKV_AT),
            ]
        )
    ]
    pairs = list(zip(mine, other, held))
    arrived = fetch(pairs[::-1], info_ref[section, 1], sems)
    for index in (2, 1, 3, 0):
        in_copies[index].start()
    w_qkv, w_out, w_up, w_down = held
    hidden_slots = u_ref.shape[0]

    if mode == "head":
        normed, scale = norm_parts(z_ref[...].astype(F32))
        channels = head_ref.shape[1]
        predicted = dot(normed.astype(BF16), head_ref[...])
        target = aim_ref[:, :channels].astype(F32)
        bucket = aim_ref[:, channels:].astype(F32)
        decay = jnp.exp(bucket * math.log(decay_base))
        loss_scale = 1.0 / math.sqrt(2 * 16 * WIN)
        grad_pred = (decay * (predicted - target) * loss_scale).astype(BF16)
        dz = norm_back(normed, scale, dot(grad_pred, head_ref[...], NT))
    else:
        dz = joined(prv_ref[...], cur_ref[...], WIN - info_ref[section, 3])
        if mode == "skip":
            dz = dz + skip_ref[...].astype(F32)
        if mode == "double":
            dz = dz + dz
    g_m = dz.astype(BF16)
    right_ref[4 + hidden_slots] = g_m
    arrived(0)
    in_copies[2].wait()
    for index in range(hidden_slots):
        dh = dot(g_m, w_down[:, index * SLOT : (index + 1) * SLOT])
        u = u_ref[index]
        square, bend, root = gelu_parts(u)
        slope = 0.5 * (1.0 + bend) + (0.5 * root) * u * (1.0 - bend * bend) * (
            1.0 + 3 * 0.044715 * square
        )
        right_ref[4 + index] = (slope * dh).astype(BF16)
    arrived(1)
    dn2 = dot(right_ref[4], w_up[:, :SLOT], NT)
    for index in range(1, hidden_slots):
        dn2 = dn2 + dot(right_ref[4 + index], w_up[:, index * SLOT : (index + 1) * SLOT], NT)
    in_copies[1].wait()
    normed, scale = norm_parts(y_ref[0])
    dy = dz + norm_back(normed, scale, dn2)
    g_a = dy.astype(BF16)
    right_ref[3] = g_a
    arrived(2)
    da = dot(g_a, w_out[...], NT).astype(BF16)

    in_copies[3].wait()
    q = qkv_ref[0].astype(F32)
    k = qkv_ref[1].astype(F32)
    q_inv, q_free = unit_rows(q)
    k_inv, k_free = unit_rows(k)
    qu = q * q_inv
    ku = k * k_inv
    qh = (logit_scale * qu).astype(BF16)
    kh = ku.astype(BF16)
    ones = jnp.ones((WIN, LANES), BF16)
    dq_parts, dk_parts = [], []
    for at in range(0, SLOT, LANES):
        kg = kh[:, at : at + LANES]
        vg = qkv_ref[2, :, at : at + LANES]
        queries = spread_heads(qh[:, at : at + LANES])
        weights = jnp.exp(dot(queries, kg, NT))
        probs = weights / dot(weights.astype(BF16), ones)
        probs_low = probs.astype(BF16)
        grads = spread_heads(da[:, at : at + LANES])
        dp = dot(grads, vg, NT)
        ds = (probs * (dp - dot((probs * dp).astype(BF16), ones))).astype(BF16)
        right_ref[2, :, at : at + LANES] = dot(probs_low, grads, TN).astype(BF16)
        dq_parts.append(gather_heads(dot(ds, kg)))
        dk_parts.append(dot(ds, queries, TN))
    dqh = logit_scale * jnp.concatenate(dq_parts, axis=1)
    dkh = jnp.concatenate(dk_parts, axis=1)
    dq = q_inv * (dqh - jnp.where(q_free, qu * head_sum(qu * dqh), 0.0))
    dk = k_inv * (dkh - jnp.where(k_free, ku * head_sum(ku * dkh), 0.0))
    right_ref[0] = dq.astype(BF16)
    right_ref[1] = dk.astype(BF16)
    right_goal = low_store.at[pl.ds(low_base + RIGHT_AT, RIGHT_SLOTS)]
    out_copy = pltpu.make_async_copy(right_ref, right_goal, out_sem.at[0])
    out_copy.start()
    arrived(3)
    in_copies[0].wait()
    if last:
        gx_ref[...] = g_a
    else:
        dn1 = dot(right_ref[0], w_qkv[:, :SLOT], NT)
        for index in (1, 2):
            dn1 = dn1 + dot(right_ref[index], w_qkv[:, index * SLOT : (index + 1) * SLOT], NT)
        normed, scale = norm_parts(x_ref[0].astype(F32))
        gx_ref[...] = (dy + norm_back(normed, scale, dn1)).astype(BF16)
    posted = pltpu.make_async_copy(gx_ref, low_store.at[low_base + GX_AT], out_sem.at[1])
    posted.start()
    out_copy.wait()
    posted.wait()


def pick_kernel(ranges, *refs):
    core_ref, store_ref = refs[:2]
    outs, sems = refs[3:-1], refs[-1]
    copies = []
    for index, (at, count, given) in enumerate(ranges):
        base = at + (1 - core_ref[0]) * LOW_SLOTS if given else at
        source = store_ref.at[pl.ds(base, count)]
        copies.append(pltpu.make_async_copy(source, outs[index], sems.at[index]))
        copies[-1].start()
    for copy in copies:
        copy.wait()


def weight_kernel(inner, *refs):
    info_ref, store_ref = refs[:2]
    received = refs[2:4]
    near_refs, far_refs = refs[4 : 4 + inner], refs[4 + inner : 4 + 2 * inner]
    left, right, room, sems = refs[4 + 2 * inner :]
    copies = []
    for into, at, count, got in ((left, LEFT_AT, LEFT_SLOTS, 0), (right, RIGHT_AT, RIGHT_SLOTS, 1)):
        for index in range(count):
            columns = pl.ds(index * SLOT, SLOT)
            for part in range(2):
                goal = into.at[pl.ds(part * WIN, WIN), columns]
                sem = sems.at[len(copies)]
                if part == 0:
                    source = store_ref.at[info_ref[0] * LOW_SLOTS + at + index]
                else:
                    source = received[got].at[index]
                copies.append(pltpu.make_async_copy(source, goal, sem))
                copies[-1].start()
    for copy in copies:
        copy.wait()
    width, step = room.shape
    hidden = right.shape[1] - 5 * width
    total = 4 * width + 2 * hidden
    outer = near_refs[0].shape[0]
    strip = near_refs[0].shape[1]
    split = near_refs[0].shape[2]
    for at in range(0, total, step):
        if at < 3 * width:
            first, second = left[:, :width], right[:, at : at + step]
        elif at < 4 * width:
            first, second = left[:, width : 2 * width], right[:, at : at + step]
        elif at < 4 * width + hidden:
            first, second = left[:, 2 * width : 3 * width], right[:, at : at + step]
        else:
            start = 3 * width + at - 4 * width - hidden
            first, second = right[:, 4 * width + hidden :], left[:, start : start + step]
        room[...] = dot(first, second, TN).astype(BF16)
        for distance in range(inner):
            if at < split:
                column = lax.rem(info_ref[1] + distance, inner)
            else:
                column = lax.rem(info_ref[2] + distance, outer)
            for line in range(outer):
                if at < split:
                    owner = line * inner + column
                    near_refs[distance][line, :, at : at + step] = room[
                        pl.ds(owner * strip, strip), :
                    ]
                else:
                    owner = column * inner + line
                    far_refs[distance][line, :, at - split : at - split + step] = room[
                        pl.ds(owner * strip, strip), :
                    ]


VMEM = pl.BlockSpec(memory_space=pltpu.VMEM)
SMEM = pl.BlockSpec(memory_space=pltpu.SMEM)
HBM = pl.BlockSpec(memory_space=pltpu.HBM)


def body(tokens, offsets, w_qkv, w_out, w_up, w_down, w_head, era5t, era5, flags, buckets):
    section_count = lax.axis_size("section")
    tok_count = lax.axis_size("tok")
    pair_count = section_count // 2
    half_pairs = pair_count // 2
    section_index = lax.axis_index("section")
    tok_index = lax.axis_index("tok")
    pair_index = section_index // 2
    core_index = section_index % 2
    micro_count, row_count, width = tokens.shape
    hidden = w_up.shape[2]
    mine = jnp.concatenate([w_qkv[0], w_out[0], w_up[0], w_down[0]], axis=1)

    def place(section, tok):
        return section * tok_count + tok % tok_count

    def moved(block, route):
        return lax.ppermute(block, ("section", "tok"), route)

    def hop(block, low_pair, step, tok_shift):
        middle = half_pairs - 1
        route = []
        for pair in range(pair_count - 1):
            if (pair > middle) - (pair < middle) == (low_pair > middle) - (low_pair < middle):
                for core in range(2):
                    for tok in range(tok_count):
                        low, high = 2 * pair + core, 2 * pair + 2 + core
                        origin, goal = (low, high) if step > 0 else (high, low)
                        route.append((place(origin, tok + tok_shift), place(goal, tok)))
        return moved(block, sorted(route))

    def along(block, tok_shift, sections):
        route = []
        for section in sections:
            for tok in range(tok_count):
                route.append((place(section, tok + tok_shift), place(section, tok)))
        return moved(block, route)

    def mirror(block, pairs):
        route = []
        for one in pairs:
            for goal in (pair_count - 1 - one,):
                for core in range(2):
                    for tok in range(tok_count):
                        origin = 2 * (pair_count - 1 - goal) + core
                        route.append((place(origin, tok), place(2 * goal + core, tok)))
        return moved(block, sorted(route))

    def swap(block):
        route = [
            (place(section, tok), place(section ^ 1, tok))
            for section in range(section_count)
            for tok in range(tok_count)
        ]
        return moved(block, route)

    def inner_hops(block, pair, sign):
        goal = pair_count - 1 - pair
        return [
            moved(
                block,
                sorted(
                    (place(2 * pair + core, tok + sign * index), place(2 * goal + core, tok))
                    for core in range(2)
                    for tok in range(tok_count)
                ),
            )
            for index in range(4)
        ]

    everyone = range(section_count)
    last_encoder = section_count // 2 - 1
    encoders = range(last_encoder - 1)
    decoders = range(last_encoder + 3, section_count)

    def far_along(block, blocks, limit, sign, sections):
        bit = 1
        while bit <= limit:
            inner = sections[:2] if sections[0] > 0 else sections[-2:]
            taking = [one for one in sections if bit < tok_count // 2 or one not in inner]
            shifted = along(block, sign * bit, taking)
            block = jnp.where((blocks // bit) % 2 == 1, shifted, block)
            bit *= 2
        return block

    def together(*arrays):
        return lax.optimization_barrier(arrays)

    table = lax.all_gather(offsets, "section").reshape(section_count)
    order = jnp.arange(section_count)
    before = jnp.where(order == 0, 0, jnp.roll(table, 1))
    shifts = (table - before + WIN) % WIN
    start = jnp.sum(jnp.where(order[:, None] >= order[None, :], shifts[None, :], 0), axis=1)

    other = swap(mine)

    info = jnp.stack(
        [
            shifts,
            (core_index == order % 2).astype(jnp.int32),
            (pair_index == order // 2).astype(jnp.int32),
            jnp.roll(shifts, -1),
        ],
        axis=1,
    ).astype(jnp.int32)

    weight_rooms = [
        pltpu.VMEM(weight.shape[1:], BF16) for weight in (w_qkv, w_out, w_up, w_down)
    ]
    weight_sems = pltpu.SemaphoreType.DMA((4,))
    rows_bf = jax.ShapeDtypeStruct((WIN, width), BF16)
    store_shapes = (
        jax.ShapeDtypeStruct((LOW_STORE, WIN, SLOT), BF16),
        jax.ShapeDtypeStruct((WIDE_STORE, WIN, SLOT), F32),
    )
    channels = era5.shape[2]
    hidden_slots = hidden // SLOT

    def room(count, dtype):
        return pltpu.VMEM((count, WIN, SLOT), dtype)

    params = pltpu.CompilerParams(vmem_limit_bytes=VMEM_LIMIT)

    def section_call(kernel, name, inputs, stores, rooms, sems):
        inputs = [info, *inputs]
        first = len(inputs) + 2
        result = pl.pallas_call(
            kernel,
            out_shape=store_shapes + (rows_bf,),
            in_specs=[SMEM] + [VMEM] * (len(inputs) - 1) + [HBM] * 4,
            out_specs=(HBM, HBM, VMEM),
            input_output_aliases={first: 0, first + 1: 1},
            scratch_shapes=weight_rooms
            + rooms
            + [room(1, F32), room(hidden_slots, F32), weight_sems]
            + [pltpu.SemaphoreType.DMA((count,)) for count in sems],
            compiler_params=params,
            name=name,
        )(*inputs, mine, other, *stores)
        return tuple(result[:2]), result[2]

    def forward(section, cur, nxt, skip, stores):
        if section < section_count // 2:
            mode = "plain"
        else:
            mode = "double" if section == section_count // 2 else "skip"
        return section_call(
            lambda *refs: forward_kernel(mode, section, *refs),
            "forward_" + mode,
            [cur, nxt] + ([skip] if mode == "skip" else []),
            stores,
            [room(1, BF16), room(3, BF16), room(LEFT_SLOTS, BF16)],
            (6,),
        )

    def backward(section, sources, skip, stores):
        if section == section_count - 1:
            mode = "head"
        elif section >= section_count // 2:
            mode = "plain"
        else:
            mode = "double" if section == section_count // 2 - 1 else "skip"
        return section_call(
            lambda *refs: backward_kernel(mode, section == 0, section, *refs),
            "backward_" + mode,
            [*sources] + ([skip] if mode == "skip" else []),
            stores,
            [room(1, BF16), room(3, BF16), room(RIGHT_SLOTS, BF16)],
            (4, 2),
        )

    core_scalar = core_index[None].astype(jnp.int32)

    def picked(stores, *ranges):
        result = pl.pallas_call(
            lambda *refs: pick_kernel(ranges, *refs),
            out_shape=(store_shapes[0],)
            + tuple(jax.ShapeDtypeStruct((count, WIN, SLOT), BF16) for _, count, _ in ranges),
            in_specs=[SMEM, HBM],
            out_specs=(HBM,) + (VMEM,) * len(ranges),
            input_output_aliases={1: 0},
            scratch_shapes=[pltpu.SemaphoreType.DMA((len(ranges),))],
            name="pick",
        )(core_scalar, stores[0])
        return (result[0], stores[1]), result[1:]

    def unwritten():
        return pl.pallas_call(
            lambda *refs: None,
            out_shape=store_shapes,
            out_specs=(HBM,) * 2,
            name="unwritten",
        )()

    cur = lax.dynamic_index_in_dim(tokens, core_index, 0, False)
    nxt = along(cur, 1, everyone)
    stores = unwritten()
    chosen = jnp.repeat(
        lax.dynamic_index_in_dim(flags, core_index, 0, False), row_count // flags.shape[1]
    )
    target = jnp.where(
        (chosen == 1)[:, None],
        lax.dynamic_index_in_dim(era5t, core_index, 0, False),
        lax.dynamic_index_in_dim(era5, core_index, 0, False),
    )
    bucket = lax.dynamic_index_in_dim(buckets, core_index, 0, False).astype(BF16)
    bucket = jnp.broadcast_to(bucket[:, None], target.shape)
    aim_here = jnp.stack([target, bucket])

    low_reach = start[section_count - 1 - 2 * pair_index] - start[2 * pair_index]
    high_reach = start[section_count - 2 - 2 * pair_index] - start[2 * pair_index + 1]
    reaches = [jnp.abs(low_reach), jnp.abs(high_reach)]
    reaches_seen = [
        jnp.where(pair_index < half_pairs, reaches[slot], reaches[1 - slot]) for slot in range(2)
    ]
    target_reach = start[section_count - 1]

    def cut(first, second, at):
        return lax.dynamic_slice_in_dim(jnp.concatenate([first, second], axis=0), at, WIN, 0)

    def long_shift(blocks, counts, limit, sign, sections):
        near = far_along(blocks, counts, limit, sign, sections)
        return near, along(near, sign, sections)

    def near_and_beside(blocks, count):
        near, beside = blocks[0], blocks[1]
        for index in range(1, len(blocks) - 1):
            near = jnp.where(count == index, blocks[index], near)
            beside = jnp.where(count == index, blocks[index + 1], beside)
        return near, beside

    def outer_skips(stores, held, first, second, limit, sign, sections, with_aim):
        stores, posts = picked(stores, (first, 1, False), (second, 1, False))
        post = jnp.concatenate(posts, axis=0)
        counts = [jnp.full((1, 1, width), each // WIN) for each in reaches_seen]
        if with_aim:
            post = jnp.concatenate([post, aim_here], axis=2)
            extra = jnp.full((1, 1, channels), target_reach // WIN)
            counts = [jnp.concatenate([count, extra], axis=2) for count in counts]
        post, *held = together(post, *held)
        near, beside = long_shift(
            mirror(post, outer_encoders if sign > 0 else outer_decoders),
            jnp.concatenate(counts, axis=0),
            limit,
            sign,
            sections,
        )
        rows = []
        for slot in range(2):
            here, there = near[slot, :, :width], beside[slot, :, :width]
            left = reaches_seen[slot] % WIN
            rows.append(cut(here, there, left) if sign > 0 else cut(there, here, WIN - left))
        if with_aim:
            aims = [
                cut(near[slot, :, width:], beside[slot, :, width:], target_reach % WIN)
                for slot in range(2)
            ]
            rows.append(jnp.concatenate(aims, axis=1))
        return stores, held, rows

    outer_encoders = range(half_pairs - 1)
    outer_decoders = range(half_pairs + 1, pair_count)
    skips = {}
    aim = None
    for pair in range(pair_count):
        low, high = 2 * pair, 2 * pair + 1
        stores, z_low = forward(low, cur, nxt, skips.get(low), stores)
        nxt = along(z_low, 1, everyone)
        if pair == half_pairs - 1:
            inner = inner_hops(z_low, pair, 1)
            nxt, *rows = together(nxt, *rows)
            aim = rows[2]
            for goal in range(half_pairs + 1, pair_count):
                skips[2 * goal + 1], skips[2 * goal] = rows[:2]
        stores, z_high = forward(high, z_low, nxt, skips.get(high), stores)
        if pair == half_pairs - 1:
            z_high, *inner[:2] = together(z_high, *inner[:2])
        if pair < pair_count - 1:
            nxt = hop(z_high, pair, 1, 1)
            cur = hop(z_high, pair, 1, 0)
        if pair == half_pairs - 2:
            stores, (cur, nxt), rows = outer_skips(
                stores, (cur, nxt), Z_AT, LOW_SLOTS + Z_AT, tok_count - 1, 1, decoders, True
            )
        if pair == half_pairs - 1:
            reach = start[low + 3] - start[low]
            near, beside = near_and_beside(inner, reach // WIN)
            skips[low + 3] = cut(near, beside, reach % WIN)

    skips = {}
    sources = (z_high, aim, w_head)
    for pair in range(pair_count - 1, -1, -1):
        low, high = 2 * pair, 2 * pair + 1
        stores, gx_high = backward(high, sources, skips.get(high), stores)
        prv = along(gx_high, -1, everyone)
        if pair == half_pairs:
            inner = inner_hops(gx_high, pair, -1)
            prv, *rows = together(prv, *rows)
            for goal in range(half_pairs - 1):
                skips[2 * goal], skips[2 * goal + 1] = rows
        sources = (gx_high, prv)
        stores, gx_low = backward(low, sources, skips.get(low), stores)
        if pair == half_pairs:
            gx_low, *inner[:2] = together(gx_low, *inner[:2])
        if pair > 0:
            prv = hop(gx_low, pair - 1, -1, -1)
            cur = hop(gx_low, pair - 1, -1, 0)
            sources = (cur, prv)
        if pair == half_pairs + 1:
            stores, sources, rows = outer_skips(
                stores, sources, LOW_SLOTS + GX_AT, GX_AT, tok_count - 2, -1, encoders, False
            )
        if pair == half_pairs:
            reach = start[high] - start[high - 3]
            near, beside = near_and_beside(inner, reach // WIN)
            skips[high - 3] = cut(beside, near, WIN - reach % WIN)
        if pair == half_pairs - 1:
            stores, given = picked(stores, (LEFT_AT, LEFT_SLOTS, True))
            cur, prv, left_other = together(cur, prv, swap(given[0]))
            sources = (cur, prv)

    stores, given = picked(stores, (RIGHT_AT, RIGHT_SLOTS, True))
    right_other = swap(given[0])
    total = 4 * width + 2 * hidden
    inner = 4
    outer = tok_count // inner
    strip = width // tok_count
    split = 4 * width + hidden
    tok_in, tok_out = tok_index % inner, tok_index // inner
    step = width
    parts = pl.pallas_call(
        lambda *refs: weight_kernel(inner, *refs),
        out_shape=[jax.ShapeDtypeStruct((outer, strip, split), BF16)] * inner
        + [jax.ShapeDtypeStruct((inner, strip, total - split), BF16)] * outer,
        in_specs=[SMEM] + [HBM] * 3,
        out_specs=[VMEM] * (inner + outer),
        scratch_shapes=[
            pltpu.VMEM((2 * WIN, LEFT_SLOTS * SLOT), BF16),
            pltpu.VMEM((2 * WIN, RIGHT_SLOTS * SLOT), BF16),
            pltpu.VMEM((width, step), BF16),
            pltpu.SemaphoreType.DMA((2 * (LEFT_SLOTS + RIGHT_SLOTS),)),
        ],
        compiler_params=params,
        name="weight_grads",
    )(
        jnp.stack([core_index, tok_in, tok_out]).astype(jnp.int32),
        stores[0],
        left_other,
        right_other,
    )
    near_parts, far_parts = parts[:inner], parts[inner:]

    def ring(block, distance, inside):
        route = []
        for tok in range(tok_count):
            far, near = tok // inner, tok % inner
            if inside:
                goal = far * inner + (near + distance) % inner
            else:
                goal = (far + distance) % outer * inner + near
            route.append((tok, goal))
        return lax.ppermute(block, "tok", route)

    def piece(array, index):
        return lax.dynamic_index_in_dim(array, index, 0, False)

    def first_stage(pieces, inside):
        summed = pieces[0].astype(F32)
        for distance in range(1, len(pieces)):
            summed = summed + ring(pieces[distance], distance, inside).astype(F32)
        return summed.astype(BF16)

    def second_stage(summed, position, size, inside):
        result = piece(summed, position).astype(F32)
        for distance in range(1, size):
            sent = piece(summed, (position + distance) % size)
            result = result + ring(sent, distance, inside).astype(F32)
        return result

    near_sums = first_stage(near_parts, True)
    far_sums = first_stage(far_parts, False)
    near_sums, far_sums = together(near_sums, far_sums)
    near_result = second_stage(near_sums, tok_out, outer, False)
    far_result = second_stage(far_sums, tok_in, inner, True)
    grad_qkv = near_result[:, : 3 * width][None]
    grad_out = near_result[:, 3 * width : 4 * width][None]
    grad_up = near_result[:, 4 * width :][None]
    grad_down = far_result[None]
    return (grad_qkv, grad_out, grad_up, grad_down)


def solution(mesh):
    placed = (
        P(None, "tok", None),
        P("section"),
        P("section", None, None),
        P("section", None, None),
        P("section", None, None),
        P("section", None, None),
        P(),
        P(None, "tok", None),
        P(None, "tok", None),
        P(None, "tok"),
        P(None, "tok"),
    )
    return jax.shard_map(
        body,
        mesh=mesh,
        in_specs=placed,
        out_specs=(
            P("section", "tok", None),
            P("section", "tok", None),
            P("section", "tok", None),
            P("section", "tok", None),
        ),
        check_vma=False,
    )
```
